128 devices in a mesh: dp: 4 (over x_hi, core), space: 32 (over x_lo, y, z).
Axes of the slice: x: 4 (x_hi: 2, x_lo: 2; x = x_hi * 2 + x_lo), y: 4, z: 4, core: 2. Of those that a mesh axis runs over, the one named last changes fastest.
Arguments:
- samples: bfloat16 [4, 320, 720, 512], P('dp', 'space'), may hold values from -6 to 6
- norm_gain: float32 [512], replicated, may hold values from 0.1 to 1.9
- norm_bias: float32 [512], replicated, may hold values from -3 to 3
- spectral_filter: float32 [320, 512, 722], P(None, ('dp', 'space')), may hold values from -4.5 to 4.5
Outputs:
- updated: bfloat16 [4, 320, 720, 512], P('dp', 'space')
The draws below stay inside these ranges and needn't reach their ends.
All inputs are finite; a program needn't handle non-finite values.
Results may differ from the reference program's by a relative error of at most 0.015.
Values may be sent and summed in bfloat16 or wider, within the bound.
No kernel may reach another device: no remote copies, remote signals or barrier semaphores. Data moves between devices by JAX's collectives and lax.ppermute only.
A program may use at most 192 MiB of HBM per device.

```python
import math
import jax
import jax.numpy as jnp
from jax import lax

H = 320
W = 720
C = 512
SAMPLES = 4
SPEC = 722


def block_scale(rng, shape, shards, least, largest):
    gain = 1.0
    for position, shards_of in shards:
        draws = jax.random.uniform(jax.random.fold_in(jax.random.fold_in(rng, 6), position), (shards_of,), jnp.float32, least / len(shards), largest / len(shards))
        gain = gain * jnp.repeat(jnp.exp(draws), shape[position] // shards_of).reshape((-1,) + (1,) * (len(shape) - 1 - position))
    return gain


def bell_draw(rng, dims, scale, most, cuts=(), kind=jnp.bfloat16):
    result = scale * jax.random.normal(rng, dims, jnp.float32)
    if cuts:
        result = result * block_scale(rng, dims, cuts, -0.22, 0.18)
    return jnp.clip(result, -most, most).astype(kind)


def setup_inputs(seed: int = 0) -> dict:
    arg_keys = jax.random.split(jax.random.key(seed), 5)
    samples = bell_draw(arg_keys[0], (SAMPLES, H, W, C), 1.0, 6.0, ((0, 4), (1, 32)))
    norm_gain = jnp.clip(1.0 + 0.18 * jax.random.normal(arg_keys[1], (C,), jnp.float32), 0.1, 1.9)
    norm_bias = bell_draw(arg_keys[2], (C,), 0.5, 3.0, (), jnp.float32)
    spectral_filter = bell_draw(arg_keys[3], (H, C, SPEC), 0.7, 4.5, ((1, 128),), jnp.float32)
    return dict(samples=samples, norm_gain=norm_gain, norm_bias=norm_bias, spectral_filter=spectral_filter)


def dft_tables(lat_len, lon_len):
    freqs = lon_len // 2 + 1
    lon_index = jnp.arange(lon_len, dtype=jnp.int32)
    freq_index = jnp.arange(freqs, dtype=jnp.int32)
    turns = (lon_index[:, None] * freq_index[None, :] % lon_len).astype(jnp.float32) * (2.0 * math.pi / lon_len)
    lon_scale = 1.0 / math.sqrt(lon_len)
    row_forward = (jnp.concatenate([jnp.cos(turns), -jnp.sin(turns)], axis=1) * lon_scale).astype(jnp.bfloat16)
    weights = jnp.where((freq_index == 0) | (freq_index == lon_len // 2), 1.0, 2.0).astype(jnp.float32)
    row_inverse = (jnp.concatenate([weights[:, None] * jnp.cos(turns).T, -weights[:, None] * jnp.sin(turns).T], axis=0) * lon_scale).astype(jnp.bfloat16)
    lat_index = jnp.arange(lat_len, dtype=jnp.int32)
    lat_turns = (lat_index[:, None] * lat_index[None, :] % lat_len).astype(jnp.float32) * (2.0 * math.pi / lat_len)
    lat_scale = 1.0 / math.sqrt(lat_len)
    col_cosine = (jnp.cos(lat_turns) * lat_scale).astype(jnp.bfloat16)
    col_sine = (jnp.sin(lat_turns) * lat_scale).astype(jnp.bfloat16)
    return (row_forward, row_inverse, col_cosine, col_sine)

def layer_norm(values, norm_gain, norm_bias):
    wide = values.astype(jnp.float32)
    center = lax.optimization_barrier(jnp.mean(wide, axis=-1, keepdims=True))
    spread = lax.optimization_barrier(jnp.mean(jnp.square(wide - center), axis=-1, keepdims=True))
    return ((wide - center) * lax.rsqrt(spread + 1e-05) * norm_gain + norm_bias).astype(jnp.bfloat16)

def reference(samples, norm_gain, norm_bias, spectral_filter):
    row_forward, row_inverse, col_cosine, col_sine = dft_tables(H, W)
    half_len = W // 2 + 1
    cos_wide = col_cosine.astype(jnp.float32)
    sin_wide = col_sine.astype(jnp.float32)
    filt_re = spectral_filter[..., :half_len]
    filt_im = spectral_filter[..., half_len:]

    def one_sample(grid):
        normed = layer_norm(grid, norm_gain, norm_bias)
        rowspec = jnp.einsum('hwc,wk->hck', normed.astype(jnp.float32), row_forward.astype(jnp.float32)).astype(jnp.bfloat16)
        spec_wide = rowspec.astype(jnp.float32)
        first = jnp.einsum('gh,hck->gck', cos_wide, spec_wide)
        second = jnp.einsum('gh,hck->gck', sin_wide, spec_wide)
        spec_re = first[..., :half_len] + second[..., half_len:]
        spec_im = first[..., half_len:] - second[..., :half_len]
        mixed = jnp.concatenate([spec_re * filt_re - spec_im * filt_im, spec_re * filt_im + spec_im * filt_re], axis=-1).astype(jnp.bfloat16)
        mixed_wide = mixed.astype(jnp.float32)
        first = jnp.einsum('gh,hck->gck', cos_wide, mixed_wide)
        second = jnp.einsum('gh,hck->gck', sin_wide, mixed_wide)
        back = jnp.concatenate([first[..., :half_len] - second[..., half_len:], first[..., half_len:] + second[..., :half_len]], axis=-1).astype(jnp.bfloat16)
        branch = jnp.einsum('hck,kw->hwc', back.astype(jnp.float32), row_inverse.astype(jnp.float32))
        return (grid.astype(jnp.float32) + branch).astype(jnp.bfloat16)
    return lax.map(one_sample, samples)
```

```python
import functools
import math

import jax
import jax.numpy as jnp
import ml_dtypes
import numpy as np
from jax import lax
from jax.experimental import pallas as pl
from jax.experimental.pallas import tpu as pltpu
from jax.sharding import PartitionSpec as P

BOTH = ("dp", "space")
WIDE = 384
HALF = WIDE // 2
MIB = 1024 * 1024


def chunk_starts(freqs):
    return range(0, freqs, HALF)


def lane_layout(start, freqs):
    lane = np.arange(WIDE)
    tail = lane >= 256
    imag = np.where(tail, lane >= 320, lane >= 128)
    freq = start + np.where(tail, 128 + lane % 64, lane % 128)
    return np.minimum(freq, freqs - 1), imag, freq < freqs


def row_tables(lon_len, start):
    freqs = lon_len // 2 + 1
    freq, imag, used = lane_layout(start, freqs)
    lon = np.arange(lon_len)
    turns = (lon[:, None] * freq[None, :] % lon_len).astype(np.float32) * np.float32(
        2.0 * math.pi / lon_len
    )
    scale = np.float32(1.0 / math.sqrt(lon_len))
    wave = np.where(imag, -np.sin(turns), np.cos(turns)) * used
    weight = np.where((freq == 0) | (freq == lon_len // 2), 1.0, 2.0).astype(np.float32)
    forward = (wave * scale).astype(ml_dtypes.bfloat16)
    inverse = (wave * weight * scale).astype(ml_dtypes.bfloat16)
    return forward, inverse


def column_tables(lat_len, chan_part):
    lat = np.arange(lat_len)
    turns = (lat[:, None] * lat[None, :] % lat_len).astype(np.float32) * np.float32(
        2.0 * math.pi / lat_len
    )
    scale = np.float32(1.0 / math.sqrt(lat_len))
    size = chan_part * lat_len
    forward = np.zeros((chan_part, lat_len, 2, lat_len, chan_part), np.float32)
    for chan in range(chan_part):
        forward[chan, :, 0, :, chan] = np.cos(turns) * scale
        forward[chan, :, 1, :, chan] = np.sin(turns) * scale
    inverse = forward.transpose(3, 4, 2, 0, 1).reshape(size, 2 * size)
    forward = forward.reshape(size, 2 * size)
    return forward.astype(ml_dtypes.bfloat16), inverse.astype(ml_dtypes.bfloat16)


def swap_parts(values):
    tail = values[:, 256:]
    return jnp.concatenate(
        [values[:, 128:256], values[:, :128], pltpu.roll(tail, 64, axis=1)], axis=1
    )


def imag_lanes(shape):
    lane = lax.broadcasted_iota(jnp.int32, shape, len(shape) - 1)
    return ((lane >= 128) & (lane < 256)) | (lane >= 320)


def first_half(shape):
    return lax.broadcasted_iota(jnp.int32, shape, 1) < 4


def pre_kernel(x_ref, gain_ref, bias_ref, table_ref, out_ref):
    specs = []
    for row in range(2):
        wide = x_ref[row].astype(jnp.float32)
        center = jnp.mean(wide, axis=-1, keepdims=True)
        wide = wide - center
        spread = jnp.mean(jnp.square(wide), axis=-1, keepdims=True)
        normed = (wide * lax.rsqrt(spread + 1e-05) * gain_ref[...] + bias_ref[...]).astype(
            jnp.bfloat16
        )
        spec = lax.dot_general(
            normed, table_ref[...], (((0,), (0,)), ((), ())), preferred_element_type=jnp.float32
        )
        specs.append(spec.reshape(spec.shape[0] // 8, 8, WIDE))
    top = first_half(specs[0].shape)
    low = jnp.where(top, specs[0], pltpu.roll(specs[1], 4, axis=1)).astype(jnp.bfloat16)
    high = jnp.where(top, pltpu.roll(specs[0], 4, axis=1), specs[1]).astype(jnp.bfloat16)
    out_ref[:, 0, 0] = low
    out_ref[:, 1, 0] = high


def pre(grid, gain, bias, table):
    rows, lon_len, channels = grid.shape
    out = pl.pallas_call(
        pre_kernel,
        grid=(rows // 2,),
        in_specs=[
            pl.BlockSpec((2, lon_len, channels), lambda i: (i, 0, 0)),
            pl.BlockSpec((1, channels), lambda i: (0, 0)),
            pl.BlockSpec((1, channels), lambda i: (0, 0)),
            pl.BlockSpec((lon_len, WIDE), lambda i: (0, 0)),
        ],
        out_specs=pl.BlockSpec((channels // 8, 2, 1, 8, WIDE), lambda i: (0, 0, i, 0, 0)),
        out_shape=jax.ShapeDtypeStruct((channels // 8, 2, rows // 2, 8, WIDE), jnp.bfloat16),
        compiler_params=pltpu.CompilerParams(vmem_limit_bytes=40 * MIB),
        cost_estimate=pl.CostEstimate(
            flops=2 * rows * lon_len * channels * WIDE,
            bytes_accessed=2 * rows * channels * (lon_len + WIDE),
            transcendentals=rows * lon_len,
        ),
        name="row_forward",
    )(grid, gain, bias, table)
    return out.reshape(channels // 4, rows // 2, 8, WIDE)


def mid_kernel(x_ref, filt_ref, forward_ref, inverse_ref, out_ref, x_both, mixed):
    size = x_both.shape[0] // 2
    rows = x_ref[...].astype(jnp.float32).reshape(size, WIDE)
    imag = imag_lanes(rows.shape)
    turned = swap_parts(rows)
    x_both[:size] = rows.astype(jnp.bfloat16)
    x_both[size:] = jnp.where(imag, -turned, turned).astype(jnp.bfloat16)
    lat_len = size // 4
    for chan in range(4):
        part = pl.ds(chan * lat_len, lat_len)
        spec = jnp.dot(forward_ref[part], x_both[...], preferred_element_type=jnp.float32)
        both = filt_ref[0, part] * spec + filt_ref[1, part] * swap_parts(spec)
        turned = swap_parts(both)
        mixed[part] = both.astype(jnp.bfloat16)
        mixed[pl.ds(size + chan * lat_len, lat_len)] = jnp.where(
            imag_lanes(both.shape), turned, -turned
        ).astype(jnp.bfloat16)
    back = jnp.dot(inverse_ref[...], mixed[...], preferred_element_type=jnp.float32)
    out_ref[...] = back.reshape(out_ref.shape).astype(jnp.bfloat16)


def mid(slab, filt, forward, inverse, samples):
    devices, pairs, eight, _ = slab.shape
    spaces = devices // samples
    size = spaces * pairs * eight
    block = pl.BlockSpec((spaces, pairs, eight, WIDE), lambda s: (s, 0, 0, 0))
    return pl.pallas_call(
        mid_kernel,
        grid=(samples,),
        in_specs=[
            block,
            pl.BlockSpec((2, size, WIDE), lambda s: (0, 0, 0)),
            pl.BlockSpec((size, 2 * size), lambda s: (0, 0)),
            pl.BlockSpec((size, 2 * size), lambda s: (0, 0)),
        ],
        out_specs=block,
        out_shape=jax.ShapeDtypeStruct(slab.shape, jnp.bfloat16),
        scratch_shapes=[
            pltpu.VMEM((2 * size, WIDE), jnp.bfloat16),
            pltpu.VMEM((2 * size, WIDE), jnp.bfloat16),
        ],
        compiler_params=pltpu.CompilerParams(vmem_limit_bytes=56 * MIB),
        cost_estimate=pl.CostEstimate(
            flops=samples * 8 * size * size * WIDE,
            bytes_accessed=4 * samples * size * WIDE + 8 * size * (WIDE + size),
            transcendentals=0,
        ),
        name="columns",
    )(slab, filt, forward, inverse)


def post_kernel(back_ref, x_ref, table_ref, out_ref):
    first = back_ref[:, 0, 0].astype(jnp.float32)
    second = back_ref[:, 1, 0].astype(jnp.float32)
    top = first_half(first.shape)
    rows = (
        jnp.where(top, first, pltpu.roll(second, 4, axis=1)),
        jnp.where(top, pltpu.roll(first, 4, axis=1), second),
    )
    for row in range(2):
        spec = rows[row].reshape(first.shape[0] * 8, WIDE).astype(jnp.bfloat16)
        branch = lax.dot_general(
            table_ref[...], spec, (((1,), (1,)), ((), ())), preferred_element_type=jnp.float32
        )
        out_ref[row] = (x_ref[row].astype(jnp.float32) + branch).astype(jnp.bfloat16)


def post(back, grid, table):
    rows, lon_len, channels = grid.shape
    block = pl.BlockSpec((2, lon_len, channels), lambda i: (i, 0, 0))
    return pl.pallas_call(
        post_kernel,
        grid=(rows // 2,),
        in_specs=[
            pl.BlockSpec((channels // 8, 2, 1, 8, WIDE), lambda i: (0, 0, i, 0, 0)),
            block,
            pl.BlockSpec((lon_len, WIDE), lambda i: (0, 0)),
        ],
        out_specs=block,
        out_shape=jax.ShapeDtypeStruct(grid.shape, jnp.bfloat16),
        compiler_params=pltpu.CompilerParams(vmem_limit_bytes=40 * MIB),
        cost_estimate=pl.CostEstimate(
            flops=2 * rows * lon_len * channels * WIDE,
            bytes_accessed=2 * rows * channels * (2 * lon_len + WIDE),
            transcendentals=0,
        ),
        name="row_inverse",
    )(back.reshape(channels // 8, 2, rows // 2, 8, WIDE), grid, table)


def filter_chunk(filt, start):
    freqs = filt.shape[-1] // 2
    by_chan = filt.transpose(1, 0, 2).reshape(-1, 2 * freqs)

    def lanes(first):
        stop = min(start + HALF, freqs)
        taken = by_chan[:, first + start : first + stop]
        return jnp.pad(taken, ((0, 0), (0, HALF - taken.shape[1])))

    real, imag = lanes(0), lanes(freqs)

    def lay(one, two):
        return jnp.concatenate([one[:, :128], two[:, :128], one[:, 128:], two[:, 128:]], axis=1)

    return jnp.stack([lay(real, real), lay(-imag, imag)])


def swap_devices(blocks):
    return lax.all_to_all(blocks, BOTH, split_axis=0, concat_axis=0, tiled=True)


def shards(samples, norm_gain, norm_bias, spectral_filter):
    grid = samples[0]
    rows, lon_len, channels = grid.shape
    dp_count = lax.axis_size("dp")
    lat_len = rows * lax.axis_size("space")
    starts = chunk_starts(lon_len // 2 + 1)
    tables = [row_tables(lon_len, start) for start in starts]
    forward, inverse = column_tables(lat_len, spectral_filter.shape[1])
    gain, bias = norm_gain[None], norm_bias[None]
    slabs = [swap_devices(pre(grid, gain, bias, jnp.asarray(table[0]))) for table in tables]
    backs = [
        swap_devices(
            mid(
                slab,
                filter_chunk(spectral_filter, start),
                jnp.asarray(forward),
                jnp.asarray(inverse),
                dp_count,
            )
        )
        for slab, start in zip(slabs, starts)
    ]
    for back, table in zip(backs, tables):
        grid = post(back, grid, jnp.asarray(table[1]))
    return grid[None]


def solution(mesh):
    placed = (P("dp", "space", None, None), P(), P(), P(None, BOTH, None))
    return jax.shard_map(
        shards, mesh=mesh, in_specs=placed, out_specs=P("dp", "space", None, None), check_vma=False
    )
```

```python
import functools
import math

import jax
import jax.numpy as jnp
import ml_dtypes
import numpy as np
from jax import lax
from jax.experimental import pallas as pl
from jax.experimental.pallas import tpu as pltpu
from jax.sharding import PartitionSpec as P

BOTH = ("dp", "space")
LANES = 128
FIRST = 256
MIB = 1024 * 1024
VMEM = 62 * MIB


def chunks(freqs):
    rest = -(-(freqs - FIRST) // LANES) * LANES
    return ((0, 2 * FIRST), (FIRST, 2 * rest))


def row_tables(lon_len, start, wide):
    freqs = lon_len // 2 + 1
    lane = np.arange(wide)
    imag = lane // LANES % 2 == 1
    freq = start + lane // (2 * LANES) * LANES + lane % LANES
    used = freq < freqs
    freq = np.minimum(freq, freqs - 1)
    lon = np.arange(lon_len)
    turns = (lon[:, None] * freq[None, :] % lon_len).astype(np.float32) * np.float32(
        2.0 * math.pi / lon_len
    )
    scale = np.float32(1.0 / math.sqrt(lon_len))
    wave = np.where(imag, -np.sin(turns), np.cos(turns)) * used
    weight = np.where((freq == 0) | (freq == lon_len // 2), 1.0, 2.0).astype(np.float32)
    forward = (wave * scale).astype(ml_dtypes.bfloat16)
    inverse = (wave * weight * scale).astype(ml_dtypes.bfloat16)
    return forward, inverse


def column_tables(lat_len, chan_part):
    lat = np.arange(lat_len)
    turns = (lat[:, None] * lat[None, :] % lat_len).astype(np.float32) * np.float32(
        2.0 * math.pi / lat_len
    )
    scale = np.float32(1.0 / math.sqrt(lat_len))
    size = chan_part * lat_len
    forward = np.zeros((chan_part, lat_len, 2, lat_len, chan_part), np.float32)
    for chan in range(chan_part):
        forward[chan, :, 0, :, chan] = np.cos(turns) * scale
        forward[chan, :, 1, :, chan] = np.sin(turns) * scale
    inverse = forward.transpose(3, 4, 2, 0, 1).reshape(size, 2 * size)
    forward = forward.reshape(size, 2 * size)
    return forward.astype(ml_dtypes.bfloat16), inverse.astype(ml_dtypes.bfloat16)


def swap_parts(values, sign=1):
    tiles = []
    for lane in range(0, values.shape[1], 2 * LANES):
        real = values[:, lane : lane + LANES]
        imag = values[:, lane + LANES : lane + 2 * LANES]
        tiles += [imag, -real] if sign > 0 else [-imag, real]
    return jnp.concatenate(tiles, axis=1)


def first_half(shape):
    return lax.broadcasted_iota(jnp.int32, shape, 1) < 4


def pre_kernel(x_ref, gain_ref, bias_ref, table_ref, out_ref):
    specs = []
    for row in range(2):
        wide = x_ref[row].astype(jnp.float32)
        center = jnp.mean(wide, axis=-1, keepdims=True)
        wide = wide - center
        spread = jnp.mean(jnp.square(wide), axis=-1, keepdims=True)
        normed = (wide * lax.rsqrt(spread + 1e-05) * gain_ref[...] + bias_ref[...]).astype(
            jnp.bfloat16
        )
        spec = lax.dot_general(
            normed, table_ref[...], (((0,), (0,)), ((), ())), preferred_element_type=jnp.float32
        )
        specs.append(spec.reshape(spec.shape[0] // 8, 8, spec.shape[1]))
    top = first_half(specs[0].shape)
    low = jnp.where(top, specs[0], pltpu.roll(specs[1], 4, axis=1)).astype(jnp.bfloat16)
    high = jnp.where(top, pltpu.roll(specs[0], 4, axis=1), specs[1]).astype(jnp.bfloat16)
    out_ref[:, 0, 0] = low
    out_ref[:, 1, 0] = high


def pre(grid, gain, bias, table):
    rows, lon_len, channels = grid.shape
    wide = table.shape[1]
    out = pl.pallas_call(
        pre_kernel,
        grid=(rows // 2,),
        in_specs=[
            pl.BlockSpec((2, lon_len, channels), lambda i: (i, 0, 0)),
            pl.BlockSpec((1, channels), lambda i: (0, 0)),
            pl.BlockSpec((1, channels), lambda i: (0, 0)),
            pl.BlockSpec((lon_len, wide), lambda i: (0, 0)),
        ],
        out_specs=pl.BlockSpec((channels // 8, 2, 1, 8, wide), lambda i: (0, 0, i, 0, 0)),
        out_shape=jax.ShapeDtypeStruct((channels // 8, 2, rows // 2, 8, wide), jnp.bfloat16),
        compiler_params=pltpu.CompilerParams(vmem_limit_bytes=VMEM),
        cost_estimate=pl.CostEstimate(
            flops=2 * rows * lon_len * channels * wide,
            bytes_accessed=2 * rows * channels * (lon_len + wide),
            transcendentals=rows * lon_len,
        ),
        name="row_forward",
    )(grid, gain, bias, table)
    return out.reshape(channels // 4, rows // 2, 8, wide)


def mid_kernel(x_ref, filt_ref, forward_ref, inverse_ref, out_ref, x_both, mixed):
    size, wide = mixed.shape[0] // 2, mixed.shape[1]
    rows = x_ref[...].astype(jnp.float32).reshape(size, wide)
    x_both[:size] = rows.astype(jnp.bfloat16)
    x_both[size:] = swap_parts(rows).astype(jnp.bfloat16)
    lat_len = size // 4
    for chan in range(4):
        part = pl.ds(chan * lat_len, lat_len)
        spec = jnp.dot(forward_ref[part], x_both[...], preferred_element_type=jnp.float32)
        tiles = []
        for lane in range(0, wide, 2 * LANES):
            half = pl.ds(lane // 2, LANES)
            filt_re, filt_im = filt_ref[0, part, half], filt_ref[1, part, half]
            spec_re = spec[:, lane : lane + LANES]
            spec_im = spec[:, lane + LANES : lane + 2 * LANES]
            tiles.append(spec_re * filt_re - spec_im * filt_im)
            tiles.append(spec_re * filt_im + spec_im * filt_re)
        both = jnp.concatenate(tiles, axis=1)
        mixed[part] = both.astype(jnp.bfloat16)
        mixed[pl.ds(size + chan * lat_len, lat_len)] = swap_parts(both, -1).astype(jnp.bfloat16)
    back = jnp.dot(inverse_ref[...], mixed[...], preferred_element_type=jnp.float32)
    out_ref[...] = back.reshape(out_ref.shape).astype(jnp.bfloat16)


def mid(slab, filt, forward, inverse, samples):
    devices, pairs, eight, wide = slab.shape
    spaces = devices // samples
    size = spaces * pairs * eight
    block = pl.BlockSpec((spaces, pairs, eight, wide), lambda s: (s, 0, 0, 0))
    once = pl.Buffered(1)
    return pl.pallas_call(
        mid_kernel,
        grid=(samples,),
        in_specs=[
            block,
            pl.BlockSpec((2, size, wide // 2), lambda s: (0, 0, 0), pipeline_mode=once),
            pl.BlockSpec((size, 2 * size), lambda s: (0, 0), pipeline_mode=once),
            pl.BlockSpec((size, 2 * size), lambda s: (0, 0), pipeline_mode=once),
        ],
        out_specs=block,
        out_shape=jax.ShapeDtypeStruct(slab.shape, jnp.bfloat16),
        scratch_shapes=[
            pltpu.VMEM((2 * size, wide), jnp.bfloat16),
            pltpu.VMEM((2 * size, wide), jnp.bfloat16),
        ],
        compiler_params=pltpu.CompilerParams(vmem_limit_bytes=VMEM),
        cost_estimate=pl.CostEstimate(
            flops=samples * 8 * size * size * wide,
            bytes_accessed=4 * samples * size * wide + 4 * size * (wide + 2 * size),
            transcendentals=0,
        ),
        name="columns",
    )(slab, filt, forward, inverse)


def post_kernel(back_ref, x_ref, table_ref, out_ref):
    first = back_ref[:, 0, 0].astype(jnp.float32)
    second = back_ref[:, 1, 0].astype(jnp.float32)
    top = first_half(first.shape)
    rows = (
        jnp.where(top, first, pltpu.roll(second, 4, axis=1)),
        jnp.where(top, pltpu.roll(first, 4, axis=1), second),
    )
    for row in range(2):
        spec = rows[row].reshape(first.shape[0] * 8, first.shape[2]).astype(jnp.bfloat16)
        branch = lax.dot_general(
            table_ref[...], spec, (((1,), (1,)), ((), ())), preferred_element_type=jnp.float32
        )
        out_ref[row] = (x_ref[row].astype(jnp.float32) + branch).astype(jnp.bfloat16)


def post(back, grid, table):
    rows, lon_len, channels = grid.shape
    wide = table.shape[1]
    block = pl.BlockSpec((2, lon_len, channels), lambda i: (i, 0, 0))
    return pl.pallas_call(
        post_kernel,
        grid=(rows // 2,),
        in_specs=[
            pl.BlockSpec((channels // 8, 2, 1, 8, wide), lambda i: (0, 0, i, 0, 0)),
            block,
            pl.BlockSpec((lon_len, wide), lambda i: (0, 0)),
        ],
        out_specs=block,
        out_shape=jax.ShapeDtypeStruct(grid.shape, jnp.bfloat16),
        compiler_params=pltpu.CompilerParams(vmem_limit_bytes=VMEM),
        cost_estimate=pl.CostEstimate(
            flops=2 * rows * lon_len * channels * wide,
            bytes_accessed=2 * rows * channels * (2 * lon_len + wide),
            transcendentals=0,
        ),
        name="row_inverse",
    )(back.reshape(channels // 8, 2, rows // 2, 8, wide), grid, table)


def filter_chunk(filt, start, wide):
    freqs = filt.shape[-1] // 2
    stop = min(start + wide // 2, freqs)
    by_chan = filt.transpose(1, 0, 2).reshape(-1, 2 * freqs)
    parts = [by_chan[:, first + start : first + stop] for first in (0, freqs)]
    return jnp.pad(jnp.stack(parts), ((0, 0), (0, 0), (0, wide // 2 - (stop - start))))


def swap_devices(blocks):
    return lax.all_to_all(blocks, BOTH, split_axis=0, concat_axis=0, tiled=True)


def shards(samples, norm_gain, norm_bias, spectral_filter):
    grid = samples[0]
    rows, lon_len, channels = grid.shape
    dp_count = lax.axis_size("dp")
    lat_len = rows * lax.axis_size("space")
    pieces = chunks(lon_len // 2 + 1)
    tables = [row_tables(lon_len, *piece) for piece in pieces]
    forward, inverse = column_tables(lat_len, spectral_filter.shape[1])
    gain, bias = norm_gain[None], norm_bias[None]
    slabs = [swap_devices(pre(grid, gain, bias, jnp.asarray(table[0]))) for table in tables]
    backs = [
        swap_devices(
            mid(
                slab,
                filter_chunk(spectral_filter, *piece),
                jnp.asarray(forward),
                jnp.asarray(inverse),
                dp_count,
            )
        )
        for slab, piece in zip(slabs, pieces)
    ]
    for back, table in zip(backs, tables):
        grid = post(back, grid, jnp.asarray(table[1]))
    return grid[None]


def solution(mesh):
    placed = (P("dp", "space", None, None), P(), P(), P(None, BOTH, None))
    return jax.shard_map(
        shards, mesh=mesh, in_specs=placed, out_specs=P("dp", "space", None, None), check_vma=False
    )
```

```python
import functools
import math

import jax
import jax.numpy as jnp
import ml_dtypes
import numpy as np
from jax import lax
from jax.experimental import pallas as pl
from jax.experimental.pallas import tpu as pltpu
from jax.sharding import PartitionSpec as P

BOTH = ("dp", "space")
LANES = 128
WIDE = 3 * LANES
HALF = WIDE // 2
SPARE = 41
GUEST = 21
PAIRS = 5
MIB = 1024 * 1024
VMEM = 62 * MIB
ANY = pl.BlockSpec(memory_space=pl.ANY)


def lane_layout(start, freqs):
    lane = np.arange(WIDE)
    tail = lane >= 256
    imag = np.where(tail, lane >= 320, lane >= 128)
    freq = start + np.where(tail, 128 + lane % 64, lane % 128)
    return np.minimum(freq, freqs - 1), imag, freq < freqs


def row_tables(lon_len, start):
    freqs = lon_len // 2 + 1
    freq, imag, used = lane_layout(start, freqs)
    lon = np.arange(lon_len)
    turns = (lon[:, None] * freq[None, :] % lon_len).astype(np.float32) * np.float32(
        2.0 * math.pi / lon_len
    )
    scale = np.float32(1.0 / math.sqrt(lon_len))
    wave = np.where(imag, -np.sin(turns), np.cos(turns)) * used
    weight = np.where((freq == 0) | (freq == lon_len // 2), 1.0, 2.0).astype(np.float32)
    forward = (wave * scale).astype(ml_dtypes.bfloat16)
    inverse = (wave * weight * scale).astype(ml_dtypes.bfloat16)
    return forward.T, inverse


def guest_home(part):
    return part // 2 * 64 + part % 2 * GUEST


def guest_columns(table):
    guests = np.zeros((table.shape[0], 4 * LANES), table.dtype)
    for part in range(4):
        home = 2 * LANES + guest_home(part)
        width = min(GUEST, SPARE - part % 2 * GUEST)
        seat = part * LANES + SPARE
        guests[:, seat : seat + width] = table[:, home : home + width]
    return np.concatenate([table[:, : 2 * LANES], guests], axis=1)


def column_tables(spaces, rows, chan_part):
    lat_len = spaces * rows
    lat = np.arange(lat_len)
    turns = (lat[:, None] * lat[None, :] % lat_len).astype(np.float32) * np.float32(
        2.0 * math.pi / lat_len
    )
    scale = np.float32(1.0 / math.sqrt(lat_len))
    size = chan_part * lat_len
    order = lat.reshape(spaces, rows // 2, 2).transpose(1, 0, 2).reshape(-1)
    forward = np.zeros((chan_part, lat_len, 2, lat_len, chan_part), np.float32)
    for chan in range(chan_part):
        forward[chan, :, 0, :, chan] = (np.cos(turns) * scale)[:, order]
        forward[chan, :, 1, :, chan] = (np.sin(turns) * scale)[:, order]
    inverse = forward.transpose(3, 4, 2, 0, 1).reshape(size, 2 * size)
    forward = forward.reshape(size, 2 * size)
    return forward.astype(ml_dtypes.bfloat16), inverse.astype(ml_dtypes.bfloat16)


def swap_parts(values):
    tail = values[:, 2 * LANES :]
    return jnp.concatenate(
        [values[:, LANES : 2 * LANES], values[:, :LANES], pltpu.roll(tail, 64, axis=1)], axis=1
    )


def imag_lanes(shape):
    lane = lax.broadcasted_iota(jnp.int32, shape, len(shape) - 1)
    return ((lane >= LANES) & (lane < 2 * LANES)) | (lane >= 320)


def first_half(shape):
    return lax.broadcasted_iota(jnp.int32, shape, 1) < 4


def interleave(one, two):
    top = first_half(one.shape)
    return (
        jnp.where(top, one, pltpu.roll(two, 4, axis=1)),
        jnp.where(top, pltpu.roll(one, 4, axis=1), two),
    )


def normed_row(values, gain, bias):
    wide = values.astype(jnp.float32)
    center = jnp.mean(wide, axis=-1, keepdims=True)
    wide = wide - center
    spread = jnp.mean(jnp.square(wide), axis=-1, keepdims=True)
    return (wide * lax.rsqrt(spread + 1e-05) * gain + bias).astype(jnp.bfloat16)


def pair_spectra(x_ref, gain_ref, bias_ref, table):
    specs = []
    for row in range(2):
        normed = normed_row(x_ref[row], gain_ref[...], bias_ref[...])
        spec = jnp.dot(table, normed, preferred_element_type=jnp.float32).T
        specs.append(spec.reshape(spec.shape[0] // 8, 8, spec.shape[1]))
    return interleave(*specs)


def pre_kernel(x_ref, gain_ref, bias_ref, table_ref, out_ref):
    both = pair_spectra(x_ref, gain_ref, bias_ref, table_ref[...])
    for side in range(2):
        out_ref[:, side, 0] = both[side].astype(jnp.bfloat16)


def pre_packed_kernel(x_ref, gain_ref, bias_ref, table_ref, last_ref, out_ref):
    pair = pl.program_id(0)

    def main(both):
        for side in range(2):
            for tile in range(2):
                out_ref[:, side, 2 * pair + tile] = both[side][
                    :, :, tile * LANES : (tile + 1) * LANES
                ].astype(jnp.bfloat16)

    @pl.when(pair < PAIRS - 1)
    def _():
        both = pair_spectra(x_ref, gain_ref, bias_ref, table_ref[...])
        main(both)
        for side in range(2):
            out_ref[:, side, 2 * PAIRS + pair] = both[side][:, :, 2 * LANES :].astype(jnp.bfloat16)

    @pl.when(pair == PAIRS - 1)
    def _():
        both = pair_spectra(x_ref, gain_ref, bias_ref, last_ref[...])
        main(both)
        for side in range(2):
            for part in range(4):
                guest = both[side][:, :, (2 + part) * LANES : (3 + part) * LANES]
                tail = out_ref[:, side, 2 * PAIRS + part].astype(jnp.float32)
                out_ref[:, side, 2 * PAIRS + part] = (tail + guest).astype(jnp.bfloat16)


def pre(grid, gain, bias, table, packed):
    rows, lon_len, channels = grid.shape
    groups = channels // 8
    if packed:
        kernel = pre_packed_kernel
        shape = (groups, 2, 3 * PAIRS - 1, 8, LANES)
        out_spec = pl.BlockSpec(shape, lambda i: (0, 0, 0, 0, 0))
        tables = (table, guest_columns(table.T).T)
    else:
        kernel = pre_kernel
        shape = (groups, 2, PAIRS, 8, WIDE)
        out_spec = pl.BlockSpec((groups, 2, 1, 8, WIDE), lambda i: (0, 0, i, 0, 0))
        tables = (table,)
    out = pl.pallas_call(
        kernel,
        grid=(rows // 2,),
        in_specs=[
            pl.BlockSpec((2, lon_len, channels), lambda i: (i, 0, 0)),
            pl.BlockSpec((1, channels), lambda i: (0, 0)),
            pl.BlockSpec((1, channels), lambda i: (0, 0)),
        ]
        + [pl.BlockSpec(each.shape, lambda i: (0, 0)) for each in tables],
        out_specs=out_spec,
        out_shape=jax.ShapeDtypeStruct(shape, jnp.bfloat16),
        compiler_params=pltpu.CompilerParams(vmem_limit_bytes=VMEM),
        cost_estimate=pl.CostEstimate(
            flops=2 * rows * lon_len * channels * WIDE,
            bytes_accessed=2 * rows * channels * (lon_len + WIDE),
            transcendentals=rows * lon_len,
        ),
        name="row_forward",
    )(grid, gain, bias, *(jnp.asarray(each) for each in tables))
    return out.reshape(2 * groups, *shape[2:])


def guest_lanes(shape, first):
    lane = lax.broadcasted_iota(jnp.int32, shape, 1)
    return (lane >= first) & (lane < first + GUEST)


def load_pairs(x_ref, packed):
    pairs = []
    if not packed:
        for pair in range(PAIRS):
            rows = x_ref[:, pair].astype(jnp.float32)
            pairs.append(rows.reshape(rows.shape[0] * 8, WIDE))
        return pairs
    tiles = []
    for tile in range(3 * PAIRS - 1):
        rows = x_ref[:, tile].astype(jnp.float32)
        tiles.append(rows.reshape(rows.shape[0] * 8, LANES))
    tails = tiles[2 * PAIRS :]
    last = jnp.zeros_like(tails[0])
    for part in range(4):
        home = guest_home(part)
        moved = pltpu.roll(tails[part], (home - SPARE) % LANES, axis=1)
        last = jnp.where(guest_lanes(last.shape, home), moved, last)
    tails.append(last)
    for pair in range(PAIRS):
        pairs.append(jnp.concatenate([tiles[2 * pair], tiles[2 * pair + 1], tails[pair]], axis=1))
    return pairs


def store_pairs(out_ref, back, packed):
    count = back.shape[0] // PAIRS
    pairs = [back[pair * count : (pair + 1) * count] for pair in range(PAIRS)]
    if not packed:
        for pair in range(PAIRS):
            out_ref[:, pair] = pairs[pair].reshape(count // 8, 8, WIDE).astype(jnp.bfloat16)
        return
    tails = [rows[:, 2 * LANES :] for rows in pairs]
    for part in range(4):
        moved = pltpu.roll(tails[-1], (SPARE - guest_home(part)) % LANES, axis=1)
        tails[part] = jnp.where(guest_lanes(moved.shape, SPARE), moved, tails[part])
    tiles = []
    for rows in pairs:
        tiles += [rows[:, :LANES], rows[:, LANES : 2 * LANES]]
    for index, tile in enumerate(tiles + tails[:-1]):
        out_ref[:, index] = tile.reshape(count // 8, 8, LANES).astype(jnp.bfloat16)


def mid_kernel(packed, x_ref, filt_ref, forward_ref, inverse_ref, out_ref, x_both, mixed):
    size = x_both.shape[0] // 2
    count = size // PAIRS
    for pair, rows in enumerate(load_pairs(x_ref, packed)):
        turned = swap_parts(rows)
        x_both[pl.ds(pair * count, count)] = rows.astype(jnp.bfloat16)
        x_both[pl.ds(size + pair * count, count)] = jnp.where(
            imag_lanes(rows.shape), -turned, turned
        ).astype(jnp.bfloat16)
    lat_len = size // 4
    for chan in range(4):
        part = pl.ds(chan * lat_len, lat_len)
        spec = jnp.dot(forward_ref[part], x_both[...], preferred_element_type=jnp.float32)
        both = filt_ref[0, part] * spec + filt_ref[1, part] * swap_parts(spec)
        turned = swap_parts(both)
        mixed[part] = both.astype(jnp.bfloat16)
        mixed[pl.ds(size + chan * lat_len, lat_len)] = jnp.where(
            imag_lanes(both.shape), turned, -turned
        ).astype(jnp.bfloat16)
    back = jnp.dot(inverse_ref[...], mixed[...], preferred_element_type=jnp.float32)
    store_pairs(out_ref, back, packed)


def mid(slab, filt, forward, inverse, samples, packed):
    spaces = slab.shape[0] // samples
    size = forward.shape[0]
    block = pl.BlockSpec((spaces, *slab.shape[1:]), lambda s: (s, 0, 0, 0))
    once = pl.Buffered(1)
    return pl.pallas_call(
        functools.partial(mid_kernel, packed),
        grid=(samples,),
        in_specs=[
            block,
            pl.BlockSpec((2, size, WIDE), lambda s: (0, 0, 0), pipeline_mode=once),
            pl.BlockSpec((size, 2 * size), lambda s: (0, 0), pipeline_mode=once),
            pl.BlockSpec((size, 2 * size), lambda s: (0, 0), pipeline_mode=once),
        ],
        out_specs=block,
        out_shape=jax.ShapeDtypeStruct(slab.shape, jnp.bfloat16),
        scratch_shapes=[
            pltpu.VMEM((2 * size, WIDE), jnp.bfloat16),
            pltpu.VMEM((2 * size, WIDE), jnp.bfloat16),
        ],
        compiler_params=pltpu.CompilerParams(vmem_limit_bytes=VMEM),
        cost_estimate=pl.CostEstimate(
            flops=samples * 8 * size * size * WIDE,
            bytes_accessed=4 * samples * size * WIDE + 8 * size * (WIDE + size),
            transcendentals=0,
        ),
        name="columns",
    )(slab, filt, forward, inverse)


def post_kernel(packed, back_hbm, x_hbm, *refs):
    tables = refs[: 1 + packed]
    out_hbm, x_in, out, x_sem, out_sem = refs[1 + packed : 6 + packed]
    mains, main_sem, *tail_refs = refs[6 + packed :]

    def main_copy(pair):
        source = back_hbm.at[:, :, pl.ds(2 * pair, 2)] if packed else back_hbm.at[:, :, pair]
        return pltpu.make_async_copy(source, mains.at[pair], main_sem.at[pair])

    def tail_copy(pair):
        tails, tail_sem = tail_refs
        return pltpu.make_async_copy(
            back_hbm.at[:, :, 2 * PAIRS + pair], tails.at[pair], tail_sem.at[pair]
        )

    def x_copy(pair):
        return pltpu.make_async_copy(x_hbm.at[pl.ds(2 * pair, 2)], x_in.at[pair], x_sem.at[pair])

    def out_copy(pair):
        return pltpu.make_async_copy(out.at[pair], out_hbm.at[pl.ds(2 * pair, 2)], out_sem.at[pair])

    for pair in range(PAIRS):
        main_copy(pair).start()
        if packed and pair < PAIRS - 1:
            tail_copy(pair).start()
        x_copy(pair).start()
    for pair in range(PAIRS):
        main_copy(pair).wait()
        if packed and pair < PAIRS - 1:
            tail_copy(pair).wait()
        if packed:
            sides = [[mains[pair, :, side, tile] for side in range(2)] for tile in range(2)]
            for part in [pair] if pair < PAIRS - 1 else range(4):
                sides.append([tail_refs[0][part, :, side] for side in range(2)])
        else:
            sides = [[mains[pair, :, side] for side in range(2)]]
        tiles = [interleave(*(each.astype(jnp.float32) for each in both)) for both in sides]
        table = tables[packed and pair == PAIRS - 1]
        x_copy(pair).wait()
        for row in range(2):
            spec = [tile[row].reshape(tile[row].shape[0] * 8, -1) for tile in tiles]
            spec = jnp.concatenate([each.astype(jnp.bfloat16) for each in spec], axis=1)
            branch = lax.dot_general(
                table[...], spec, (((1,), (1,)), ((), ())), preferred_element_type=jnp.float32
            )
            out[pair, row] = (x_in[pair, row].astype(jnp.float32) + branch).astype(jnp.bfloat16)
        out_copy(pair).start()
    for pair in range(PAIRS):
        out_copy(pair).wait()


def post(back, grid, table, packed):
    rows, lon_len, channels = grid.shape
    groups = channels // 8
    tables = (table, guest_columns(table)) if packed else (table,)
    main = (PAIRS, groups, 2, 2, 8, LANES) if packed else (PAIRS, groups, 2, 8, WIDE)
    scratch = [
        pltpu.VMEM((PAIRS, 2, lon_len, channels), jnp.bfloat16),
        pltpu.VMEM((PAIRS, 2, lon_len, channels), jnp.bfloat16),
        pltpu.SemaphoreType.DMA((PAIRS,)),
        pltpu.SemaphoreType.DMA((PAIRS,)),
        pltpu.VMEM(main, jnp.bfloat16),
        pltpu.SemaphoreType.DMA((PAIRS,)),
    ]
    if packed:
        scratch += [
            pltpu.VMEM((PAIRS - 1, groups, 2, 8, LANES), jnp.bfloat16),
            pltpu.SemaphoreType.DMA((PAIRS - 1,)),
        ]
    return pl.pallas_call(
        functools.partial(post_kernel, packed),
        in_specs=[ANY, ANY] + [pl.BlockSpec(memory_space=pltpu.VMEM)] * len(tables),
        out_specs=ANY,
        out_shape=jax.ShapeDtypeStruct(grid.shape, jnp.bfloat16),
        scratch_shapes=scratch,
        compiler_params=pltpu.CompilerParams(vmem_limit_bytes=VMEM),
        cost_estimate=pl.CostEstimate(
            flops=2 * rows * lon_len * channels * WIDE,
            bytes_accessed=2 * rows * channels * (2 * lon_len + WIDE),
            transcendentals=0,
        ),
        name="row_inverse",
    )(
        back.reshape(groups, 2, *back.shape[1:]),
        grid,
        *(jnp.asarray(each) for each in tables),
    )


def filter_chunk(filt, start):
    freqs = filt.shape[-1] // 2
    by_chan = filt.transpose(1, 0, 2).reshape(-1, 2 * freqs)

    def lanes(first):
        stop = min(start + HALF, freqs)
        taken = by_chan[:, first + start : first + stop]
        return jnp.pad(taken, ((0, 0), (0, HALF - taken.shape[1])))

    real, imag = lanes(0), lanes(freqs)

    def lay(one, two):
        return jnp.concatenate(
            [one[:, :LANES], two[:, :LANES], one[:, LANES:], two[:, LANES:]], axis=1
        )

    return jnp.stack([lay(real, real), lay(-imag, imag)])


def swap_devices(blocks):
    return lax.all_to_all(blocks, BOTH, split_axis=0, concat_axis=0, tiled=True)


def shards(samples, norm_gain, norm_bias, spectral_filter):
    grid = samples[0]
    rows, lon_len, _ = grid.shape
    dp_count = lax.axis_size("dp")
    starts = (0, HALF)
    tables = [row_tables(lon_len, start) for start in starts]
    columns = column_tables(lax.axis_size("space"), rows, spectral_filter.shape[1])
    forward, inverse = (jnp.asarray(each) for each in columns)
    gain, bias = norm_gain[None], norm_bias[None]
    slabs = [
        swap_devices(pre(grid, gain, bias, tables[index][0], index == 1)) for index in range(2)
    ]
    backs = []
    for index in range(2):
        filt = filter_chunk(spectral_filter, starts[index])
        back = mid(slabs[index], filt, forward, inverse, dp_count, index == 1)
        backs.append(swap_devices(back))
    for index in range(2):
        grid = post(backs[index], grid, tables[index][1], index == 1)
    return grid[None]


def solution(mesh):
    placed = (P("dp", "space", None, None), P(), P(), P(None, BOTH, None))
    return jax.shard_map(
        shards, mesh=mesh, in_specs=placed, out_specs=P("dp", "space", None, None), check_vma=False
    )
```

```python
import functools
import math

import jax
import jax.numpy as jnp
import ml_dtypes
import numpy as np
from jax import lax
from jax.experimental import pallas as pl
from jax.experimental.pallas import tpu as pltpu
from jax.sharding import PartitionSpec as P

BOTH = ("dp", "space")
LANES = 128
WIDE = 3 * LANES
HALF = WIDE // 2
SPARE = 41
GUEST = 21
PAIRS = 5
MIB = 1024 * 1024
VMEM = 62 * MIB
ANY = pl.BlockSpec(memory_space=pl.ANY)


def lane_layout(start, freqs):
    lane = np.arange(WIDE)
    tail = lane >= 256
    imag = np.where(tail, lane >= 320, lane >= 128)
    freq = start + np.where(tail, 128 + lane % 64, lane % 128)
    return np.minimum(freq, freqs - 1), imag, freq < freqs


def row_tables(lon_len, start):
    freqs = lon_len // 2 + 1
    freq, imag, used = lane_layout(start, freqs)
    lon = np.arange(lon_len)
    turns = (lon[:, None] * freq[None, :] % lon_len).astype(np.float32) * np.float32(
        2.0 * math.pi / lon_len
    )
    scale = np.float32(1.0 / math.sqrt(lon_len))
    wave = np.where(imag, -np.sin(turns), np.cos(turns)) * used
    weight = np.where((freq == 0) | (freq == lon_len // 2), 1.0, 2.0).astype(np.float32)
    forward = (wave * scale).astype(ml_dtypes.bfloat16)
    inverse = (wave * weight * scale).astype(ml_dtypes.bfloat16)
    return forward.T, inverse


def guest_home(part):
    return part // 2 * 64 + part % 2 * GUEST


def guest_columns(table):
    guests = np.zeros((table.shape[0], 4 * LANES), table.dtype)
    for part in range(4):
        home = 2 * LANES + guest_home(part)
        width = min(GUEST, SPARE - part % 2 * GUEST)
        seat = part * LANES + SPARE
        guests[:, seat : seat + width] = table[:, home : home + width]
    return np.concatenate([table[:, : 2 * LANES], guests], axis=1)


def column_tables(spaces, rows, chan_part):
    lat_len = spaces * rows
    lat = np.arange(lat_len)
    turns = (lat[:, None] * lat[None, :] % lat_len).astype(np.float32) * np.float32(
        2.0 * math.pi / lat_len
    )
    scale = np.float32(1.0 / math.sqrt(lat_len))
    size = chan_part * lat_len
    order = lat.reshape(spaces, rows // 2, 2).transpose(1, 0, 2).reshape(-1)
    forward = np.zeros((chan_part, lat_len, 2, lat_len, chan_part), np.float32)
    for chan in range(chan_part):
        forward[chan, :, 0, :, chan] = (np.cos(turns) * scale)[:, order]
        forward[chan, :, 1, :, chan] = (np.sin(turns) * scale)[:, order]
    inverse = forward.transpose(3, 4, 2, 0, 1).reshape(size, 2 * size)
    forward = forward.reshape(size, 2 * size)
    return forward.astype(ml_dtypes.bfloat16), inverse.astype(ml_dtypes.bfloat16)


def swap_parts(values):
    tail = values[:, 2 * LANES :]
    return jnp.concatenate(
        [values[:, LANES : 2 * LANES], values[:, :LANES], pltpu.roll(tail, 64, axis=1)], axis=1
    )


def imag_lanes(shape):
    lane = lax.broadcasted_iota(jnp.int32, shape, len(shape) - 1)
    return ((lane >= LANES) & (lane < 2 * LANES)) | (lane >= 320)


def first_half(shape):
    return lax.broadcasted_iota(jnp.int32, shape, 1) < 4


def interleave(one, two):
    top = first_half(one.shape)
    return (
        jnp.where(top, one, pltpu.roll(two, 4, axis=1)),
        jnp.where(top, pltpu.roll(one, 4, axis=1), two),
    )


def normed_row(values, gain, bias):
    wide = values.astype(jnp.float32)
    center = jnp.mean(wide, axis=-1, keepdims=True)
    wide = wide - center
    spread = jnp.mean(jnp.square(wide), axis=-1, keepdims=True)
    return (wide * lax.rsqrt(spread + 1e-05) * gain + bias).astype(jnp.bfloat16)


def pair_spectra(x_ref, gain_ref, bias_ref, table):
    specs = []
    for row in range(2):
        normed = normed_row(x_ref[row], gain_ref[...], bias_ref[...])
        spec = jnp.dot(table, normed, preferred_element_type=jnp.float32).T
        specs.append(spec.reshape(spec.shape[0] // 8, 8, spec.shape[1]))
    return interleave(*specs)


def pre_kernel(x_ref, gain_ref, bias_ref, table_ref, out_ref):
    both = pair_spectra(x_ref, gain_ref, bias_ref, table_ref[...])
    for side in range(2):
        out_ref[:, side, 0] = both[side].astype(jnp.bfloat16)


def pre_packed_kernel(x_ref, gain_ref, bias_ref, table_ref, last_ref, out_ref):
    pair = pl.program_id(0)

    def main(both):
        for side in range(2):
            for tile in range(2):
                out_ref[:, side, 2 * pair + tile] = both[side][
                    :, :, tile * LANES : (tile + 1) * LANES
                ].astype(jnp.bfloat16)

    @pl.when(pair < PAIRS - 1)
    def _():
        both = pair_spectra(x_ref, gain_ref, bias_ref, table_ref[...])
        main(both)
        for side in range(2):
            out_ref[:, side, 2 * PAIRS + pair] = both[side][:, :, 2 * LANES :].astype(jnp.bfloat16)

    @pl.when(pair == PAIRS - 1)
    def _():
        both = pair_spectra(x_ref, gain_ref, bias_ref, last_ref[...])
        main(both)
        for side in range(2):
            for part in range(4):
                guest = both[side][:, :, (2 + part) * LANES : (3 + part) * LANES]
                tail = out_ref[:, side, 2 * PAIRS + part].astype(jnp.float32)
                out_ref[:, side, 2 * PAIRS + part] = (tail + guest).astype(jnp.bfloat16)


def pre(grid, gain, bias, table, packed):
    rows, lon_len, channels = grid.shape
    groups = channels // 8
    if packed:
        kernel = pre_packed_kernel
        shape = (groups, 2, 3 * PAIRS - 1, 8, LANES)
        out_spec = pl.BlockSpec(shape, lambda i: (0, 0, 0, 0, 0))
        tables = (table, guest_columns(table.T).T)
    else:
        kernel = pre_kernel
        shape = (groups, 2, PAIRS, 8, WIDE)
        out_spec = pl.BlockSpec((groups, 2, 1, 8, WIDE), lambda i: (0, 0, i, 0, 0))
        tables = (table,)
    out = pl.pallas_call(
        kernel,
        grid=(rows // 2,),
        in_specs=[
            pl.BlockSpec((2, lon_len, channels), lambda i: (i, 0, 0)),
            pl.BlockSpec((1, channels), lambda i: (0, 0)),
            pl.BlockSpec((1, channels), lambda i: (0, 0)),
        ]
        + [pl.BlockSpec(each.shape, lambda i: (0, 0)) for each in tables],
        out_specs=out_spec,
        out_shape=jax.ShapeDtypeStruct(shape, jnp.bfloat16),
        compiler_params=pltpu.CompilerParams(vmem_limit_bytes=VMEM),
        cost_estimate=pl.CostEstimate(
            flops=2 * rows * lon_len * channels * WIDE,
            bytes_accessed=2 * rows * channels * (lon_len + WIDE),
            transcendentals=rows * lon_len,
        ),
        name="row_forward",
    )(grid, gain, bias, *(jnp.asarray(each) for each in tables))
    return out.reshape(2 * groups, *shape[2:])


def guest_lanes(shape, first):
    lane = lax.broadcasted_iota(jnp.int32, shape, 1)
    return (lane >= first) & (lane < first + GUEST)


def load_pairs(x_ref, packed):
    pairs = []
    if not packed:
        for pair in range(PAIRS):
            rows = x_ref[:, pair].astype(jnp.float32)
            pairs.append(rows.reshape(rows.shape[0] * 8, WIDE))
        return pairs
    tiles = []
    for tile in range(3 * PAIRS - 1):
        rows = x_ref[:, tile].astype(jnp.float32)
        tiles.append(rows.reshape(rows.shape[0] * 8, LANES))
    tails = tiles[2 * PAIRS :]
    last = jnp.zeros_like(tails[0])
    for part in range(4):
        home = guest_home(part)
        moved = pltpu.roll(tails[part], (home - SPARE) % LANES, axis=1)
        last = jnp.where(guest_lanes(last.shape, home), moved, last)
    tails.append(last)
    for pair in range(PAIRS):
        pairs.append(jnp.concatenate([tiles[2 * pair], tiles[2 * pair + 1], tails[pair]], axis=1))
    return pairs


def store_pairs(out_ref, back, packed):
    count = back.shape[0] // PAIRS
    pairs = [back[pair * count : (pair + 1) * count] for pair in range(PAIRS)]
    if not packed:
        for pair in range(PAIRS):
            out_ref[:, pair] = pairs[pair].reshape(count // 8, 8, WIDE).astype(jnp.bfloat16)
        return
    tails = [rows[:, 2 * LANES :] for rows in pairs]
    for part in range(4):
        moved = pltpu.roll(tails[-1], (SPARE - guest_home(part)) % LANES, axis=1)
        tails[part] = jnp.where(guest_lanes(moved.shape, SPARE), moved, tails[part])
    tiles = []
    for rows in pairs:
        tiles += [rows[:, :LANES], rows[:, LANES : 2 * LANES]]
    for index, tile in enumerate(tiles + tails[:-1]):
        out_ref[:, index] = tile.reshape(count // 8, 8, LANES).astype(jnp.bfloat16)


def mid_kernel(packed, x_ref, filt_ref, forward_ref, inverse_ref, out_ref, x_both, mixed):
    size = x_both.shape[0] // 2
    count = size // PAIRS
    for pair, rows in enumerate(load_pairs(x_ref, packed)):
        turned = swap_parts(rows)
        x_both[pl.ds(pair * count, count)] = rows.astype(jnp.bfloat16)
        x_both[pl.ds(size + pair * count, count)] = jnp.where(
            imag_lanes(rows.shape), -turned, turned
        ).astype(jnp.bfloat16)
    lat_len = size // 4
    for chan in range(4):
        part = pl.ds(chan * lat_len, lat_len)
        spec = jnp.dot(forward_ref[part], x_both[...], preferred_element_type=jnp.float32)
        both = filt_ref[0, part] * spec + filt_ref[1, part] * swap_parts(spec)
        turned = swap_parts(both)
        mixed[part] = both.astype(jnp.bfloat16)
        mixed[pl.ds(size + chan * lat_len, lat_len)] = jnp.where(
            imag_lanes(both.shape), turned, -turned
        ).astype(jnp.bfloat16)
    back = jnp.dot(inverse_ref[...], mixed[...], preferred_element_type=jnp.float32)
    store_pairs(out_ref, back, packed)


def mid(slab, filt, forward, inverse, samples, packed):
    spaces = slab.shape[0] // samples
    size = forward.shape[0]
    block = pl.BlockSpec((spaces, *slab.shape[1:]), lambda s: (s, 0, 0, 0))
    once = pl.Buffered(1)
    return pl.pallas_call(
        functools.partial(mid_kernel, packed),
        grid=(samples,),
        in_specs=[
            block,
            pl.BlockSpec((2, size, WIDE), lambda s: (0, 0, 0), pipeline_mode=once),
            pl.BlockSpec((size, 2 * size), lambda s: (0, 0), pipeline_mode=once),
            pl.BlockSpec((size, 2 * size), lambda s: (0, 0), pipeline_mode=once),
        ],
        out_specs=block,
        out_shape=jax.ShapeDtypeStruct(slab.shape, jnp.bfloat16),
        scratch_shapes=[
            pltpu.VMEM((2 * size, WIDE), jnp.bfloat16),
            pltpu.VMEM((2 * size, WIDE), jnp.bfloat16),
        ],
        compiler_params=pltpu.CompilerParams(vmem_limit_bytes=VMEM),
        cost_estimate=pl.CostEstimate(
            flops=samples * 8 * size * size * WIDE,
            bytes_accessed=4 * samples * size * WIDE + 8 * size * (WIDE + size),
            transcendentals=0,
        ),
        name="columns",
    )(slab, filt, forward, inverse)


def post_kernel(packed, back_hbm, x_hbm, *refs):
    tables = refs[: 1 + packed]
    out_hbm, x_in, out, x_sem, out_sem = refs[1 + packed : 6 + packed]
    mains, main_sem, *tail_refs = refs[6 + packed :]

    def main_copy(pair):
        source = back_hbm.at[:, :, pl.ds(2 * pair, 2)] if packed else back_hbm.at[:, :, pair]
        return pltpu.make_async_copy(source, mains.at[pair], main_sem.at[pair])

    def tail_copy(pair):
        tails, tail_sem = tail_refs
        return pltpu.make_async_copy(
            back_hbm.at[:, :, 2 * PAIRS + pair], tails.at[pair], tail_sem.at[pair]
        )

    def x_copy(pair):
        return pltpu.make_async_copy(x_hbm.at[pl.ds(2 * pair, 2)], x_in.at[pair], x_sem.at[pair])

    def out_copy(pair):
        return pltpu.make_async_copy(out.at[pair], out_hbm.at[pl.ds(2 * pair, 2)], out_sem.at[pair])

    for pair in range(PAIRS):
        main_copy(pair).start()
        if packed and pair < PAIRS - 1:
            tail_copy(pair).start()
        x_copy(pair).start()
    for pair in range(PAIRS):
        main_copy(pair).wait()
        if packed and pair < PAIRS - 1:
            tail_copy(pair).wait()
        if packed:
            sides = [[mains[pair, :, side, tile] for side in range(2)] for tile in range(2)]
            for part in [pair] if pair < PAIRS - 1 else range(4):
                sides.append([tail_refs[0][part, :, side] for side in range(2)])
        else:
            sides = [[mains[pair, :, side] for side in range(2)]]
        tiles = [interleave(*(each.astype(jnp.float32) for each in both)) for both in sides]
        table = tables[packed and pair == PAIRS - 1]
        x_copy(pair).wait()
        for row in range(2):
            spec = [tile[row].reshape(tile[row].shape[0] * 8, -1) for tile in tiles]
            spec = jnp.concatenate([each.astype(jnp.bfloat16) for each in spec], axis=1)
            branch = lax.dot_general(
                table[...], spec, (((1,), (1,)), ((), ())), preferred_element_type=jnp.float32
            )
            out[pair, row] = (x_in[pair, row].astype(jnp.float32) + branch).astype(jnp.bfloat16)
        out_copy(pair).start()
    for pair in range(PAIRS):
        out_copy(pair).wait()


def post(back, grid, table, packed):
    rows, lon_len, channels = grid.shape
    groups = channels // 8
    tables = (table, guest_columns(table)) if packed else (table,)
    main = (PAIRS, groups, 2, 2, 8, LANES) if packed else (PAIRS, groups, 2, 8, WIDE)
    scratch = [
        pltpu.VMEM((PAIRS, 2, lon_len, channels), jnp.bfloat16),
        pltpu.VMEM((PAIRS, 2, lon_len, channels), jnp.bfloat16),
        pltpu.SemaphoreType.DMA((PAIRS,)),
        pltpu.SemaphoreType.DMA((PAIRS,)),
        pltpu.VMEM(main, jnp.bfloat16),
        pltpu.SemaphoreType.DMA((PAIRS,)),
    ]
    if packed:
        scratch += [
            pltpu.VMEM((PAIRS - 1, groups, 2, 8, LANES), jnp.bfloat16),
            pltpu.SemaphoreType.DMA((PAIRS - 1,)),
        ]
    return pl.pallas_call(
        functools.partial(post_kernel, packed),
        in_specs=[ANY, ANY] + [pl.BlockSpec(memory_space=pltpu.VMEM)] * len(tables),
        out_specs=ANY,
        out_shape=jax.ShapeDtypeStruct(grid.shape, jnp.bfloat16),
        scratch_shapes=scratch,
        compiler_params=pltpu.CompilerParams(vmem_limit_bytes=VMEM - MIB),
        cost_estimate=pl.CostEstimate(
            flops=2 * rows * lon_len * channels * WIDE,
            bytes_accessed=2 * rows * channels * (2 * lon_len + WIDE),
            transcendentals=0,
        ),
        name="row_inverse",
    )(
        back.reshape(groups, 2, *back.shape[1:]),
        grid,
        *(jnp.asarray(each) for each in tables),
    )


def filter_chunk(filt, start):
    freqs = filt.shape[-1] // 2
    by_chan = filt.transpose(1, 0, 2).reshape(-1, 2 * freqs)

    def lanes(first):
        stop = min(start + HALF, freqs)
        taken = by_chan[:, first + start : first + stop]
        return jnp.pad(taken, ((0, 0), (0, HALF - taken.shape[1])))

    real, imag = lanes(0), lanes(freqs)

    def lay(one, two):
        return jnp.concatenate(
            [one[:, :LANES], two[:, :LANES], one[:, LANES:], two[:, LANES:]], axis=1
        )

    return jnp.stack([lay(real, real), lay(-imag, imag)])


def swap_devices(blocks):
    return lax.all_to_all(blocks, BOTH, split_axis=0, concat_axis=0, tiled=True)


def shards(samples, norm_gain, norm_bias, spectral_filter):
    grid = samples[0]
    rows, lon_len, _ = grid.shape
    dp_count = lax.axis_size("dp")
    starts = (0, HALF)
    tables = [row_tables(lon_len, start) for start in starts]
    columns = column_tables(lax.axis_size("space"), rows, spectral_filter.shape[1])
    forward, inverse = (jnp.asarray(each) for each in columns)
    gain, bias = norm_gain[None], norm_bias[None]
    spectra = [pre(grid, gain, bias, tables[index][0], index == 1) for index in range(2)]
    filts = [filter_chunk(spectral_filter, start) for start in starts]
    spectra[1], filts = lax.optimization_barrier((spectra[1], filts))
    slabs = [swap_devices(each) for each in spectra]
    backs = []
    for index in range(2):
        back = mid(slabs[index], filts[index], forward, inverse, dp_count, index == 1)
        backs.append(swap_devices(back))
    for index in range(2):
        grid = post(backs[index], grid, tables[index][1], index == 1)
    return grid[None]


def solution(mesh):
    placed = (P("dp", "space", None, None), P(), P(), P(None, BOTH, None))
    return jax.shard_map(
        shards, mesh=mesh, in_specs=placed, out_specs=P("dp", "space", None, None), check_vma=False
    )
```

```python
import functools
import math

import jax
import jax.numpy as jnp
import ml_dtypes
import numpy as np
from jax import lax
from jax.experimental import pallas as pl
from jax.experimental.pallas import tpu as pltpu
from jax.sharding import PartitionSpec as P

BOTH = ("dp", "space")
LANES = 128
WIDE = 3 * LANES
HALF = WIDE // 2
SPARE = 41
GUEST = 21
PAIRS = 5
MIB = 1024 * 1024
VMEM = 62 * MIB
ANY = pl.BlockSpec(memory_space=pl.ANY)


def lane_layout(start, freqs):
    lane = np.arange(WIDE)
    tail = lane >= 256
    imag = np.where(tail, lane >= 320, lane >= 128)
    freq = start + np.where(tail, 128 + lane % 64, lane % 128)
    return np.minimum(freq, freqs - 1), imag, freq < freqs


def row_tables(lon_len, start):
    freqs = lon_len // 2 + 1
    freq, imag, used = lane_layout(start, freqs)
    lon = np.arange(lon_len)
    turns = (lon[:, None] * freq[None, :] % lon_len).astype(np.float32) * np.float32(
        2.0 * math.pi / lon_len
    )
    scale = np.float32(1.0 / math.sqrt(lon_len))
    wave = np.where(imag, -np.sin(turns), np.cos(turns)) * used
    weight = np.where((freq == 0) | (freq == lon_len // 2), 1.0, 2.0).astype(np.float32)
    forward = (wave * scale).astype(ml_dtypes.bfloat16)
    inverse = (wave * weight * scale).astype(ml_dtypes.bfloat16)
    return forward.T, inverse


def guest_home(part):
    return part // 2 * 64 + part % 2 * GUEST


def guest_columns(table):
    guests = np.zeros((table.shape[0], 4 * LANES), table.dtype)
    for part in range(4):
        home = 2 * LANES + guest_home(part)
        width = min(GUEST, SPARE - part % 2 * GUEST)
        seat = part * LANES + SPARE
        guests[:, seat : seat + width] = table[:, home : home + width]
    return np.concatenate([table[:, : 2 * LANES], guests], axis=1)


def column_tables(spaces, rows, chan_part):
    lat_len = spaces * rows
    lat = np.arange(lat_len)
    turns = (lat[:, None] * lat[None, :] % lat_len).astype(np.float32) * np.float32(
        2.0 * math.pi / lat_len
    )
    scale = np.float32(1.0 / math.sqrt(lat_len))
    size = chan_part * lat_len
    order = lat.reshape(spaces, rows // 2, 2).transpose(1, 0, 2).reshape(-1)
    forward = np.zeros((chan_part, lat_len, 2, lat_len, chan_part), np.float32)
    for chan in range(chan_part):
        forward[chan, :, 0, :, chan] = (np.cos(turns) * scale)[:, order]
        forward[chan, :, 1, :, chan] = (np.sin(turns) * scale)[:, order]
    inverse = forward.transpose(3, 4, 2, 0, 1).reshape(size, 2 * size)
    forward = forward.reshape(size, 2 * size)
    return forward.astype(ml_dtypes.bfloat16), inverse.astype(ml_dtypes.bfloat16)


def swap_parts(values):
    tail = values[:, 2 * LANES :]
    return jnp.concatenate(
        [values[:, LANES : 2 * LANES], values[:, :LANES], pltpu.roll(tail, 64, axis=1)], axis=1
    )


def imag_lanes(shape):
    lane = lax.broadcasted_iota(jnp.int32, shape, len(shape) - 1)
    return ((lane >= LANES) & (lane < 2 * LANES)) | (lane >= 320)


def first_half(shape):
    return lax.broadcasted_iota(jnp.int32, shape, 1) < 4


def interleave(one, two):
    top = first_half(one.shape)
    return (
        jnp.where(top, one, pltpu.roll(two, 4, axis=1)),
        jnp.where(top, pltpu.roll(one, 4, axis=1), two),
    )


def normed_row(values, gain, bias):
    wide = values.astype(jnp.float32)
    center = jnp.mean(wide, axis=-1, keepdims=True)
    wide = wide - center
    spread = jnp.mean(jnp.square(wide), axis=-1, keepdims=True)
    return (wide * lax.rsqrt(spread + 1e-05) * gain + bias).astype(jnp.bfloat16)


def pair_spectra(x_ref, gain_ref, bias_ref, table):
    specs = []
    for row in range(2):
        normed = normed_row(x_ref[row], gain_ref[...], bias_ref[...])
        spec = jnp.dot(table, normed, preferred_element_type=jnp.float32).T
        specs.append(spec.reshape(spec.shape[0] // 8, 8, spec.shape[1]))
    return interleave(*specs)


def pre_kernel(x_hbm, gain_ref, bias_ref, table_hbm, out_hbm, x_in, out, table, even, odd, *sems):
    x_sem, out_sem, table_sem = sems
    tables = pltpu.make_async_copy(table_hbm, table, table_sem)
    groups = out.shape[1]

    def pair_in(pair):
        return pltpu.make_async_copy(x_hbm.at[pl.ds(2 * pair, 2)], x_in.at[pair], x_sem.at[pair])

    def pair_out(pair):
        return pltpu.make_async_copy(out.at[pair], out_hbm.at[:, :, pair], out_sem.at[pair])

    def spectrum(normed):
        return jnp.dot(table[...], normed[...], preferred_element_type=jnp.float32)

    def arrived(pair):
        pair_in(pair).wait()
        if pair + 2 < PAIRS:
            pair_in(pair + 2).start()

    pair_in(0).start()
    tables.start()
    pair_in(1).start()
    arrived(0)
    even[...] = normed_row(x_in[0, 0], gain_ref[...], bias_ref[...])
    tables.wait()
    for pair in range(PAIRS):
        if pair + 1 < PAIRS:
            arrived(pair + 1)
        first = spectrum(even)
        odd[...] = normed_row(x_in[pair, 1], gain_ref[...], bias_ref[...])
        second = spectrum(odd)
        if pair + 1 < PAIRS:
            even[...] = normed_row(x_in[pair + 1, 0], gain_ref[...], bias_ref[...])
        both = interleave(*(each.T.reshape(groups, 8, WIDE) for each in (first, second)))
        for side in range(2):
            out[pair, :, side] = both[side].astype(jnp.bfloat16)
        pair_out(pair).start()
    for pair in range(PAIRS):
        pair_out(pair).wait()


def pre_packed_kernel(x_ref, gain_ref, bias_ref, table_ref, last_ref, out_ref):
    pair = pl.program_id(0)

    def main(both):
        for side in range(2):
            for tile in range(2):
                out_ref[:, side, 2 * pair + tile] = both[side][
                    :, :, tile * LANES : (tile + 1) * LANES
                ].astype(jnp.bfloat16)

    @pl.when(pair < PAIRS - 1)
    def _():
        both = pair_spectra(x_ref, gain_ref, bias_ref, table_ref[...])
        main(both)
        for side in range(2):
            out_ref[:, side, 2 * PAIRS + pair] = both[side][:, :, 2 * LANES :].astype(jnp.bfloat16)

    @pl.when(pair == PAIRS - 1)
    def _():
        both = pair_spectra(x_ref, gain_ref, bias_ref, last_ref[...])
        main(both)
        for side in range(2):
            for part in range(4):
                guest = both[side][:, :, (2 + part) * LANES : (3 + part) * LANES]
                tail = out_ref[:, side, 2 * PAIRS + part].astype(jnp.float32)
                out_ref[:, side, 2 * PAIRS + part] = (tail + guest).astype(jnp.bfloat16)


def pre(grid, gain, bias, table, packed):
    rows, lon_len, channels = grid.shape
    groups = channels // 8
    small = pl.BlockSpec((1, channels), lambda *i: (0, 0))
    tables = (jnp.asarray(np.ascontiguousarray(table)),)
    if packed:
        kernel, steps = pre_packed_kernel, (PAIRS,)
        shape = (groups, 2, 3 * PAIRS - 1, 8, LANES)
        tables += (jnp.asarray(np.ascontiguousarray(guest_columns(table.T).T)),)
        table_specs = [pl.BlockSpec(each.shape, lambda i: (0, 0)) for each in tables]
        x_spec = pl.BlockSpec((2, lon_len, channels), lambda i: (i, 0, 0))
        out_spec = pl.BlockSpec(shape, lambda i: (0, 0, 0, 0, 0))
        scratch = []
    else:
        kernel, steps = pre_kernel, ()
        shape = (groups, 2, PAIRS, 8, WIDE)
        table_specs, x_spec, out_spec = [ANY], ANY, ANY
        scratch = [
            pltpu.VMEM((PAIRS, 2, lon_len, channels), jnp.bfloat16),
            pltpu.VMEM((PAIRS, groups, 2, 8, WIDE), jnp.bfloat16),
            pltpu.VMEM(table.shape, jnp.bfloat16),
            pltpu.VMEM((lon_len, channels), jnp.bfloat16),
            pltpu.VMEM((lon_len, channels), jnp.bfloat16),
            pltpu.SemaphoreType.DMA((PAIRS,)),
            pltpu.SemaphoreType.DMA((PAIRS,)),
            pltpu.SemaphoreType.DMA,
        ]
    out = pl.pallas_call(
        kernel,
        grid=steps,
        in_specs=[x_spec, small, small] + table_specs,
        out_specs=out_spec,
        out_shape=jax.ShapeDtypeStruct(shape, jnp.bfloat16),
        scratch_shapes=scratch,
        compiler_params=pltpu.CompilerParams(vmem_limit_bytes=VMEM),
        cost_estimate=pl.CostEstimate(
            flops=2 * rows * lon_len * channels * WIDE,
            bytes_accessed=2 * rows * channels * (lon_len + WIDE),
            transcendentals=rows * lon_len,
        ),
        name="row_forward",
    )(grid, gain, bias, *tables)
    return out.reshape(2 * groups, *shape[2:])


def guest_lanes(shape, first):
    lane = lax.broadcasted_iota(jnp.int32, shape, 1)
    return (lane >= first) & (lane < first + GUEST)


def load_pairs(x_ref, packed):
    pairs = []
    if not packed:
        for pair in range(PAIRS):
            rows = x_ref[:, pair].astype(jnp.float32)
            pairs.append(rows.reshape(rows.shape[0] * 8, WIDE))
        return pairs
    tiles = []
    for tile in range(3 * PAIRS - 1):
        rows = x_ref[:, tile].astype(jnp.float32)
        tiles.append(rows.reshape(rows.shape[0] * 8, LANES))
    tails = tiles[2 * PAIRS :]
    last = jnp.zeros_like(tails[0])
    for part in range(4):
        home = guest_home(part)
        moved = pltpu.roll(tails[part], (home - SPARE) % LANES, axis=1)
        last = jnp.where(guest_lanes(last.shape, home), moved, last)
    tails.append(last)
    for pair in range(PAIRS):
        pairs.append(jnp.concatenate([tiles[2 * pair], tiles[2 * pair + 1], tails[pair]], axis=1))
    return pairs


def store_pairs(out_ref, back, packed):
    count = back.shape[0] // PAIRS
    pairs = [back[pair * count : (pair + 1) * count] for pair in range(PAIRS)]
    if not packed:
        for pair in range(PAIRS):
            out_ref[:, pair] = pairs[pair].reshape(count // 8, 8, WIDE).astype(jnp.bfloat16)
        return
    tails = [rows[:, 2 * LANES :] for rows in pairs]
    for part in range(4):
        moved = pltpu.roll(tails[-1], (SPARE - guest_home(part)) % LANES, axis=1)
        tails[part] = jnp.where(guest_lanes(moved.shape, SPARE), moved, tails[part])
    tiles = []
    for rows in pairs:
        tiles += [rows[:, :LANES], rows[:, LANES : 2 * LANES]]
    for index, tile in enumerate(tiles + tails[:-1]):
        out_ref[:, index] = tile.reshape(count // 8, 8, LANES).astype(jnp.bfloat16)


def mid_kernel(packed, x_ref, filt_ref, forward_ref, inverse_ref, out_ref, x_both, mixed):
    size = x_both.shape[0] // 2
    count = size // PAIRS
    for pair, rows in enumerate(load_pairs(x_ref, packed)):
        turned = swap_parts(rows)
        x_both[pl.ds(pair * count, count)] = rows.astype(jnp.bfloat16)
        x_both[pl.ds(size + pair * count, count)] = jnp.where(
            imag_lanes(rows.shape), -turned, turned
        ).astype(jnp.bfloat16)
    lat_len = size // 4
    for chan in range(4):
        part = pl.ds(chan * lat_len, lat_len)
        spec = jnp.dot(forward_ref[part], x_both[...], preferred_element_type=jnp.float32)
        both = filt_ref[0, part] * spec + filt_ref[1, part] * swap_parts(spec)
        turned = swap_parts(both)
        mixed[part] = both.astype(jnp.bfloat16)
        mixed[pl.ds(size + chan * lat_len, lat_len)] = jnp.where(
            imag_lanes(both.shape), turned, -turned
        ).astype(jnp.bfloat16)
    back = jnp.dot(inverse_ref[...], mixed[...], preferred_element_type=jnp.float32)
    store_pairs(out_ref, back, packed)


def mid(slab, filt, forward, inverse, samples, packed):
    spaces = slab.shape[0] // samples
    size = forward.shape[0]
    block = pl.BlockSpec((spaces, *slab.shape[1:]), lambda s: (s, 0, 0, 0))
    once = pl.Buffered(1)
    return pl.pallas_call(
        functools.partial(mid_kernel, packed),
        grid=(samples,),
        in_specs=[
            block,
            pl.BlockSpec((2, size, WIDE), lambda s: (0, 0, 0), pipeline_mode=once),
            pl.BlockSpec((size, 2 * size), lambda s: (0, 0), pipeline_mode=once),
            pl.BlockSpec((size, 2 * size), lambda s: (0, 0), pipeline_mode=once),
        ],
        out_specs=block,
        out_shape=jax.ShapeDtypeStruct(slab.shape, jnp.bfloat16),
        scratch_shapes=[
            pltpu.VMEM((2 * size, WIDE), jnp.bfloat16),
            pltpu.VMEM((2 * size, WIDE), jnp.bfloat16),
        ],
        compiler_params=pltpu.CompilerParams(vmem_limit_bytes=VMEM),
        cost_estimate=pl.CostEstimate(
            flops=samples * 8 * size * size * WIDE,
            bytes_accessed=4 * samples * size * WIDE + 8 * size * (WIDE + size),
            transcendentals=0,
        ),
        name="columns",
    )(slab, filt, forward, inverse)


def post_kernel(packed, back_hbm, x_hbm, table_hbm, out_hbm, x_in, out, slab, spec, table, *sems):
    x_sem, out_sem, main_sem, tail_sem, table_sem = sems
    groups = slab.shape[0]
    tables = pltpu.make_async_copy(table_hbm, table, table_sem)

    def inputs(pair):
        mains = pl.ds(2 * pair, 2) if packed else pair
        copies = [
            pltpu.make_async_copy(
                back_hbm.at[:, :, mains], slab.at[:, :, mains], main_sem.at[pair]
            )
        ]
        if packed and pair < PAIRS - 1:
            tail = 2 * PAIRS + pair
            copies.append(
                pltpu.make_async_copy(
                    back_hbm.at[:, :, tail], slab.at[:, :, tail], tail_sem.at[pair]
                )
            )
        copies.append(
            pltpu.make_async_copy(x_hbm.at[pl.ds(2 * pair, 2)], x_in.at[pair], x_sem.at[pair])
        )
        return copies

    def output(pair, row):
        return pltpu.make_async_copy(
            out.at[pair, row], out_hbm.at[2 * pair + row], out_sem.at[pair, row]
        )

    def rows_of(tile):
        both = (slab[:, side, tile].astype(jnp.float32) for side in range(2))
        return [each.reshape(groups * 8, each.shape[2]) for each in interleave(*both)]

    def tail_rows(pair):
        if pair < PAIRS - 1:
            return rows_of(2 * PAIRS + pair)
        last = [jnp.zeros((groups * 8, LANES), jnp.float32)] * 2
        for part in range(4):
            home = guest_home(part)
            for row, guest in enumerate(rows_of(2 * PAIRS + part)):
                moved = pltpu.roll(guest, (home - SPARE) % LANES, axis=1)
                last[row] = jnp.where(guest_lanes(moved.shape, home), moved, last[row])
        return last

    for copy in [tables] + inputs(0) + inputs(1):
        copy.start()
    for pair in range(PAIRS):
        for copy in inputs(pair):
            copy.wait()
        if pair == 0:
            tables.wait()
        if pair + 2 < PAIRS:
            for copy in inputs(pair + 2):
                copy.start()
        if packed:
            tiles = [rows_of(2 * pair), rows_of(2 * pair + 1), tail_rows(pair)]
        else:
            tiles = [rows_of(pair)]
        for row in range(2):
            lane = 0
            for tile in tiles:
                wide = tile[row].shape[1]
                spec[row, :, lane : lane + wide] = tile[row].astype(jnp.bfloat16)
                lane += wide
        for row in range(2):
            branch = lax.dot_general(
                table[...], spec[row], (((1,), (1,)), ((), ())), preferred_element_type=jnp.float32
            )
            out[pair, row] = (x_in[pair, row].astype(jnp.float32) + branch).astype(jnp.bfloat16)
            output(pair, row).start()
    for pair in range(PAIRS):
        for row in range(2):
            output(pair, row).wait()


def post(back, grid, table, packed):
    rows, lon_len, channels = grid.shape
    groups = channels // 8
    back = back.reshape(groups, 2, *back.shape[1:])
    return pl.pallas_call(
        functools.partial(post_kernel, packed),
        in_specs=[ANY] * 3,
        out_specs=ANY,
        out_shape=jax.ShapeDtypeStruct(grid.shape, jnp.bfloat16),
        scratch_shapes=[
            pltpu.VMEM((PAIRS, 2, lon_len, channels), jnp.bfloat16),
            pltpu.VMEM((PAIRS, 2, lon_len, channels), jnp.bfloat16),
            pltpu.VMEM(back.shape, jnp.bfloat16),
            pltpu.VMEM((2, channels, WIDE), jnp.bfloat16),
            pltpu.VMEM((lon_len, WIDE), jnp.bfloat16),
            pltpu.SemaphoreType.DMA((PAIRS,)),
            pltpu.SemaphoreType.DMA((PAIRS, 2)),
            pltpu.SemaphoreType.DMA((PAIRS,)),
            pltpu.SemaphoreType.DMA((PAIRS,)),
            pltpu.SemaphoreType.DMA,
        ],
        compiler_params=pltpu.CompilerParams(vmem_limit_bytes=VMEM),
        cost_estimate=pl.CostEstimate(
            flops=2 * rows * lon_len * channels * WIDE,
            bytes_accessed=2 * rows * channels * (2 * lon_len + WIDE),
            transcendentals=0,
        ),
        name="row_inverse",
    )(back, grid, jnp.asarray(table))


def filter_chunk(filt, start):
    freqs = filt.shape[-1] // 2
    by_chan = filt.transpose(1, 0, 2).reshape(-1, 2 * freqs)

    def lanes(first):
        stop = min(start + HALF, freqs)
        taken = by_chan[:, first + start : first + stop]
        return jnp.pad(taken, ((0, 0), (0, HALF - taken.shape[1])))

    real, imag = lanes(0), lanes(freqs)

    def lay(one, two):
        return jnp.concatenate(
            [one[:, :LANES], two[:, :LANES], one[:, LANES:], two[:, LANES:]], axis=1
        )

    return jnp.stack([lay(real, real), lay(-imag, imag)])


def swap_devices(blocks):
    return lax.all_to_all(blocks, BOTH, split_axis=0, concat_axis=0, tiled=True)


def shards(samples, norm_gain, norm_bias, spectral_filter):
    grid = samples[0]
    rows, lon_len, _ = grid.shape
    dp_count = lax.axis_size("dp")
    starts = (0, HALF)
    tables = [row_tables(lon_len, start) for start in starts]
    columns = column_tables(lax.axis_size("space"), rows, spectral_filter.shape[1])
    forward, inverse = (jnp.asarray(each) for each in columns)
    gain, bias = norm_gain[None], norm_bias[None]
    spectra = [pre(grid, gain, bias, tables[index][0], index == 1) for index in range(2)]
    filts = [filter_chunk(spectral_filter, start) for start in starts]
    spectra[1], filts = lax.optimization_barrier((spectra[1], filts))
    slabs = [swap_devices(each) for each in spectra]
    backs = []
    for index in range(2):
        back = mid(slabs[index], filts[index], forward, inverse, dp_count, index == 1)
        backs.append(swap_devices(back))
    for index in range(2):
        grid = post(backs[index], grid, tables[index][1], index == 1)
    return grid[None]


def solution(mesh):
    placed = (P("dp", "space", None, None), P(), P(), P(None, BOTH, None))
    return jax.shard_map(
        shards, mesh=mesh, in_specs=placed, out_specs=P("dp", "space", None, None), check_vma=False
    )
```

```python
import functools
import math

import jax
import jax.numpy as jnp
import ml_dtypes
import numpy as np
from jax import lax
from jax.experimental import pallas as pl
from jax.experimental.pallas import tpu as pltpu
from jax.sharding import PartitionSpec as P

BOTH = ("dp", "space")
LANES = 128
WIDE = 3 * LANES
HALF = WIDE // 2
SPARE = 41
GUEST = 21
PAIRS = 5
MIB = 1024 * 1024
VMEM = 62 * MIB
ANY = pl.BlockSpec(memory_space=pl.ANY)


def lane_layout(start, freqs):
    lane = np.arange(WIDE)
    tail = lane >= 256
    imag = np.where(tail, lane >= 320, lane >= 128)
    freq = start + np.where(tail, 128 + lane % 64, lane % 128)
    return np.minimum(freq, freqs - 1), imag, freq < freqs


def row_tables(lon_len, start):
    freqs = lon_len // 2 + 1
    freq, imag, used = lane_layout(start, freqs)
    lon = np.arange(lon_len)
    turns = (lon[:, None] * freq[None, :] % lon_len).astype(np.float32) * np.float32(
        2.0 * math.pi / lon_len
    )
    scale = np.float32(1.0 / math.sqrt(lon_len))
    wave = np.where(imag, -np.sin(turns), np.cos(turns)) * used
    weight = np.where((freq == 0) | (freq == lon_len // 2), 1.0, 2.0).astype(np.float32)
    forward = (wave * scale).astype(ml_dtypes.bfloat16)
    inverse = (wave * weight * scale).astype(ml_dtypes.bfloat16)
    return forward.T, inverse


def guest_home(part):
    return part // 2 * 64 + part % 2 * GUEST


def guest_columns(table):
    guests = np.zeros((table.shape[0], 4 * LANES), table.dtype)
    for part in range(4):
        home = 2 * LANES + guest_home(part)
        width = min(GUEST, SPARE - part % 2 * GUEST)
        seat = part * LANES + SPARE
        guests[:, seat : seat + width] = table[:, home : home + width]
    return np.concatenate([table[:, : 2 * LANES], guests], axis=1)


def column_tables(spaces, rows, chan_part):
    lat_len = spaces * rows
    lat = np.arange(lat_len)
    turns = (lat[:, None] * lat[None, :] % lat_len).astype(np.float32) * np.float32(
        2.0 * math.pi / lat_len
    )
    scale = np.float32(1.0 / math.sqrt(lat_len))
    size = chan_part * lat_len
    order = lat.reshape(spaces, rows // 2, 2).transpose(1, 0, 2).reshape(-1)
    forward = np.zeros((chan_part, lat_len, 2, lat_len, chan_part), np.float32)
    for chan in range(chan_part):
        forward[chan, :, 0, :, chan] = (np.cos(turns) * scale)[:, order]
        forward[chan, :, 1, :, chan] = (np.sin(turns) * scale)[:, order]
    inverse = forward.transpose(3, 4, 2, 0, 1).reshape(size, 2 * size)
    forward = forward.reshape(size, 2 * size)
    return forward.astype(ml_dtypes.bfloat16), inverse.astype(ml_dtypes.bfloat16)


def swap_parts(values):
    tail = values[:, 2 * LANES :]
    return jnp.concatenate(
        [values[:, LANES : 2 * LANES], values[:, :LANES], pltpu.roll(tail, 64, axis=1)], axis=1
    )


def imag_lanes(shape):
    lane = lax.broadcasted_iota(jnp.int32, shape, len(shape) - 1)
    return ((lane >= LANES) & (lane < 2 * LANES)) | (lane >= 320)


def first_half(shape):
    return lax.broadcasted_iota(jnp.int32, shape, 1) < 4


def interleave(one, two):
    top = first_half(one.shape)
    return (
        jnp.where(top, one, pltpu.roll(two, 4, axis=1)),
        jnp.where(top, pltpu.roll(one, 4, axis=1), two),
    )


def normed_row(values, gain, bias):
    wide = values.astype(jnp.float32)
    center = jnp.mean(wide, axis=-1, keepdims=True)
    wide = wide - center
    spread = jnp.mean(jnp.square(wide), axis=-1, keepdims=True)
    return (wide * lax.rsqrt(spread + 1e-05) * gain + bias).astype(jnp.bfloat16)


def pair_spectra(x_ref, gain_ref, bias_ref, table):
    specs = []
    for row in range(2):
        normed = normed_row(x_ref[row], gain_ref[...], bias_ref[...])
        spec = jnp.dot(table, normed, preferred_element_type=jnp.float32).T
        specs.append(spec.reshape(spec.shape[0] // 8, 8, spec.shape[1]))
    return interleave(*specs)


def pre_kernel(x_ref, gain_ref, bias_ref, table_ref, out_ref):
    both = pair_spectra(x_ref, gain_ref, bias_ref, table_ref[...])
    for side in range(2):
        out_ref[:, side, 0] = both[side].astype(jnp.bfloat16)


def pre_packed_kernel(x_ref, gain_ref, bias_ref, table_ref, last_ref, out_ref):
    pair = pl.program_id(0)

    def main(both):
        for side in range(2):
            for tile in range(2):
                out_ref[:, side, 2 * pair + tile] = both[side][
                    :, :, tile * LANES : (tile + 1) * LANES
                ].astype(jnp.bfloat16)

    @pl.when(pair < PAIRS - 1)
    def _():
        both = pair_spectra(x_ref, gain_ref, bias_ref, table_ref[...])
        main(both)
        for side in range(2):
            out_ref[:, side, 2 * PAIRS + pair] = both[side][:, :, 2 * LANES :].astype(jnp.bfloat16)

    @pl.when(pair == PAIRS - 1)
    def _():
        both = pair_spectra(x_ref, gain_ref, bias_ref, last_ref[...])
        main(both)
        for side in range(2):
            for part in range(4):
                guest = both[side][:, :, (2 + part) * LANES : (3 + part) * LANES]
                tail = out_ref[:, side, 2 * PAIRS + part].astype(jnp.float32)
                out_ref[:, side, 2 * PAIRS + part] = (tail + guest).astype(jnp.bfloat16)


def pre(grid, gain, bias, table, packed):
    rows, lon_len, channels = grid.shape
    groups = channels // 8
    if packed:
        kernel = pre_packed_kernel
        shape = (groups, 2, 3 * PAIRS - 1, 8, LANES)
        out_spec = pl.BlockSpec(shape, lambda i: (0, 0, 0, 0, 0))
        tables = (table, guest_columns(table.T).T)
    else:
        kernel = pre_kernel
        shape = (groups, 2, PAIRS, 8, WIDE)
        out_spec = pl.BlockSpec((groups, 2, 1, 8, WIDE), lambda i: (0, 0, i, 0, 0))
        tables = (table,)
    out = pl.pallas_call(
        kernel,
        grid=(rows // 2,),
        in_specs=[
            pl.BlockSpec((2, lon_len, channels), lambda i: (i, 0, 0)),
            pl.BlockSpec((1, channels), lambda i: (0, 0)),
            pl.BlockSpec((1, channels), lambda i: (0, 0)),
        ]
        + [pl.BlockSpec(each.shape, lambda i: (0, 0)) for each in tables],
        out_specs=out_spec,
        out_shape=jax.ShapeDtypeStruct(shape, jnp.bfloat16),
        compiler_params=pltpu.CompilerParams(vmem_limit_bytes=VMEM),
        cost_estimate=pl.CostEstimate(
            flops=2 * rows * lon_len * channels * WIDE,
            bytes_accessed=2 * rows * channels * (lon_len + WIDE),
            transcendentals=rows * lon_len,
        ),
        name="row_forward",
    )(grid, gain, bias, *(jnp.asarray(each) for each in tables))
    return out.reshape(2 * groups, *shape[2:])


def guest_lanes(shape, first):
    lane = lax.broadcasted_iota(jnp.int32, shape, 1)
    return (lane >= first) & (lane < first + GUEST)


def load_pairs(x_ref, packed):
    pairs = []
    if not packed:
        for pair in range(PAIRS):
            rows = x_ref[:, pair].astype(jnp.float32)
            pairs.append(rows.reshape(rows.shape[0] * 8, WIDE))
        return pairs
    tiles = []
    for tile in range(3 * PAIRS - 1):
        rows = x_ref[:, tile].astype(jnp.float32)
        tiles.append(rows.reshape(rows.shape[0] * 8, LANES))
    tails = tiles[2 * PAIRS :]
    last = jnp.zeros_like(tails[0])
    for part in range(4):
        home = guest_home(part)
        moved = pltpu.roll(tails[part], (home - SPARE) % LANES, axis=1)
        last = jnp.where(guest_lanes(last.shape, home), moved, last)
    tails.append(last)
    for pair in range(PAIRS):
        pairs.append(jnp.concatenate([tiles[2 * pair], tiles[2 * pair + 1], tails[pair]], axis=1))
    return pairs


def store_pairs(out_ref, back, packed):
    count = back.shape[0] // PAIRS
    pairs = [back[pair * count : (pair + 1) * count] for pair in range(PAIRS)]
    if not packed:
        for pair in range(PAIRS):
            out_ref[:, pair] = pairs[pair].reshape(count // 8, 8, WIDE).astype(jnp.bfloat16)
        return
    tails = [rows[:, 2 * LANES :] for rows in pairs]
    for part in range(4):
        moved = pltpu.roll(tails[-1], (SPARE - guest_home(part)) % LANES, axis=1)
        tails[part] = jnp.where(guest_lanes(moved.shape, SPARE), moved, tails[part])
    tiles = []
    for rows in pairs:
        tiles += [rows[:, :LANES], rows[:, LANES : 2 * LANES]]
    for index, tile in enumerate(tiles + tails[:-1]):
        out_ref[:, index] = tile.reshape(count // 8, 8, LANES).astype(jnp.bfloat16)


def mid_kernel(packed, x_ref, filt_ref, forward_ref, inverse_ref, out_ref, x_both, mixed):
    size = x_both.shape[0] // 2
    count = size // PAIRS
    for pair, rows in enumerate(load_pairs(x_ref, packed)):
        turned = swap_parts(rows)
        x_both[pl.ds(pair * count, count)] = rows.astype(jnp.bfloat16)
        x_both[pl.ds(size + pair * count, count)] = jnp.where(
            imag_lanes(rows.shape), -turned, turned
        ).astype(jnp.bfloat16)
    lat_len = size // 4
    for chan in range(4):
        part = pl.ds(chan * lat_len, lat_len)
        spec = jnp.dot(forward_ref[part], x_both[...], preferred_element_type=jnp.float32)
        both = filt_ref[0, part] * spec + filt_ref[1, part] * swap_parts(spec)
        turned = swap_parts(both)
        mixed[part] = both.astype(jnp.bfloat16)
        mixed[pl.ds(size + chan * lat_len, lat_len)] = jnp.where(
            imag_lanes(both.shape), turned, -turned
        ).astype(jnp.bfloat16)
    back = jnp.dot(inverse_ref[...], mixed[...], preferred_element_type=jnp.float32)
    store_pairs(out_ref, back, packed)


def mid(slab, filt, forward, inverse, samples, packed):
    spaces = slab.shape[0] // samples
    size = forward.shape[0]
    block = pl.BlockSpec((spaces, *slab.shape[1:]), lambda s: (s, 0, 0, 0))
    once = pl.Buffered(1)
    return pl.pallas_call(
        functools.partial(mid_kernel, packed),
        grid=(samples,),
        in_specs=[
            block,
            pl.BlockSpec((2, size, WIDE), lambda s: (0, 0, 0), pipeline_mode=once),
            pl.BlockSpec((size, 2 * size), lambda s: (0, 0), pipeline_mode=once),
            pl.BlockSpec((size, 2 * size), lambda s: (0, 0), pipeline_mode=once),
        ],
        out_specs=block,
        out_shape=jax.ShapeDtypeStruct(slab.shape, jnp.bfloat16),
        scratch_shapes=[
            pltpu.VMEM((2 * size, WIDE), jnp.bfloat16),
            pltpu.VMEM((2 * size, WIDE), jnp.bfloat16),
        ],
        compiler_params=pltpu.CompilerParams(vmem_limit_bytes=VMEM),
        cost_estimate=pl.CostEstimate(
            flops=samples * 8 * size * size * WIDE,
            bytes_accessed=4 * samples * size * WIDE + 8 * size * (WIDE + size),
            transcendentals=0,
        ),
        name="columns",
    )(slab, filt, forward, inverse)


def post_kernel(packed, back_hbm, x_hbm, table, out_hbm, x_in, out, slab, spec, *sems):
    x_sem, out_sem, main_sem, tail_sem = sems
    groups = slab.shape[0]

    def inputs(pair):
        mains = pl.ds(2 * pair, 2) if packed else pair
        copies = [
            pltpu.make_async_copy(
                back_hbm.at[:, :, mains], slab.at[:, :, mains], main_sem.at[pair]
            )
        ]
        if packed and pair < PAIRS - 1:
            tail = 2 * PAIRS + pair
            copies.append(
                pltpu.make_async_copy(
                    back_hbm.at[:, :, tail], slab.at[:, :, tail], tail_sem.at[pair]
                )
            )
        copies.append(
            pltpu.make_async_copy(x_hbm.at[pl.ds(2 * pair, 2)], x_in.at[pair], x_sem.at[pair])
        )
        return copies

    def output(pair):
        return pltpu.make_async_copy(out.at[pair], out_hbm.at[pl.ds(2 * pair, 2)], out_sem.at[pair])

    def rows_of(tile):
        both = (slab[:, side, tile].astype(jnp.float32) for side in range(2))
        return [each.reshape(groups * 8, each.shape[2]) for each in interleave(*both)]

    def tail_rows(pair):
        if pair < PAIRS - 1:
            return rows_of(2 * PAIRS + pair)
        last = [jnp.zeros((groups * 8, LANES), jnp.float32)] * 2
        for part in range(4):
            home = guest_home(part)
            for row, guest in enumerate(rows_of(2 * PAIRS + part)):
                moved = pltpu.roll(guest, (home - SPARE) % LANES, axis=1)
                last[row] = jnp.where(guest_lanes(moved.shape, home), moved, last[row])
        return last

    for copy in inputs(0) + inputs(1):
        copy.start()
    for pair in range(PAIRS):
        for copy in inputs(pair):
            copy.wait()
        if pair + 2 < PAIRS:
            for copy in inputs(pair + 2):
                copy.start()
        if packed:
            tiles = [rows_of(2 * pair), rows_of(2 * pair + 1), tail_rows(pair)]
        else:
            tiles = [rows_of(pair)]
        for row in range(2):
            lane = 0
            for tile in tiles:
                wide = tile[row].shape[1]
                spec[row, :, lane : lane + wide] = tile[row].astype(jnp.bfloat16)
                lane += wide
        for row in range(2):
            branch = lax.dot_general(
                table[...], spec[row], (((1,), (1,)), ((), ())), preferred_element_type=jnp.float32
            )
            out[pair, row] = (x_in[pair, row].astype(jnp.float32) + branch).astype(jnp.bfloat16)
        output(pair).start()
    for pair in range(PAIRS):
        output(pair).wait()


def post(back, grid, table, packed):
    rows, lon_len, channels = grid.shape
    groups = channels // 8
    back = back.reshape(groups, 2, *back.shape[1:])
    return pl.pallas_call(
        functools.partial(post_kernel, packed),
        in_specs=[ANY, ANY, pl.BlockSpec(memory_space=pltpu.VMEM)],
        out_specs=ANY,
        out_shape=jax.ShapeDtypeStruct(grid.shape, jnp.bfloat16),
        scratch_shapes=[
            pltpu.VMEM((PAIRS, 2, lon_len, channels), jnp.bfloat16),
            pltpu.VMEM((PAIRS, 2, lon_len, channels), jnp.bfloat16),
            pltpu.VMEM(back.shape, jnp.bfloat16),
            pltpu.VMEM((2, channels, WIDE), jnp.bfloat16),
        ]
        + [pltpu.SemaphoreType.DMA((PAIRS,))] * 4,
        compiler_params=pltpu.CompilerParams(vmem_limit_bytes=VMEM - MIB),
        cost_estimate=pl.CostEstimate(
            flops=2 * rows * lon_len * channels * WIDE,
            bytes_accessed=2 * rows * channels * (2 * lon_len + WIDE),
            transcendentals=0,
        ),
        name="row_inverse",
    )(back, grid, jnp.asarray(table))


def filter_chunk(filt, start):
    freqs = filt.shape[-1] // 2
    by_chan = filt.transpose(1, 0, 2).reshape(-1, 2 * freqs)

    def lanes(first):
        stop = min(start + HALF, freqs)
        taken = by_chan[:, first + start : first + stop]
        return jnp.pad(taken, ((0, 0), (0, HALF - taken.shape[1])))

    real, imag = lanes(0), lanes(freqs)

    def lay(one, two):
        return jnp.concatenate(
            [one[:, :LANES], two[:, :LANES], one[:, LANES:], two[:, LANES:]], axis=1
        )

    return jnp.stack([lay(real, real), lay(-imag, imag)])


def swap_devices(blocks):
    return lax.all_to_all(blocks, BOTH, split_axis=0, concat_axis=0, tiled=True)


def shards(samples, norm_gain, norm_bias, spectral_filter):
    grid = samples[0]
    rows, lon_len, _ = grid.shape
    dp_count = lax.axis_size("dp")
    starts = (0, HALF)
    tables = [row_tables(lon_len, start) for start in starts]
    columns = column_tables(lax.axis_size("space"), rows, spectral_filter.shape[1])
    forward, inverse = (jnp.asarray(each) for each in columns)
    gain, bias = norm_gain[None], norm_bias[None]
    spectra = [pre(grid, gain, bias, tables[index][0], index == 1) for index in range(2)]
    filts = [filter_chunk(spectral_filter, start) for start in starts]
    spectra[1], filts = lax.optimization_barrier((spectra[1], filts))
    slabs = [swap_devices(each) for each in spectra]
    backs = []
    for index in range(2):
        back = mid(slabs[index], filts[index], forward, inverse, dp_count, index == 1)
        backs.append(swap_devices(back))
    for index in range(2):
        grid = post(backs[index], grid, tables[index][1], index == 1)
    return grid[None]


def solution(mesh):
    placed = (P("dp", "space", None, None), P(), P(), P(None, BOTH, None))
    return jax.shard_map(
        shards, mesh=mesh, in_specs=placed, out_specs=P("dp", "space", None, None), check_vma=False
    )
```

```python
import functools
import math

import jax
import jax.numpy as jnp
import ml_dtypes
import numpy as np
from jax import lax
from jax.experimental import pallas as pl
from jax.experimental.pallas import tpu as pltpu
from jax.sharding import PartitionSpec as P

BOTH = ("dp", "space")
LANES = 128
WIDE = 3 * LANES
HALF = WIDE // 2
SPARE = 41
GUEST = 21
PAIRS = 5
MIB = 1024 * 1024
VMEM = 62 * MIB
ANY = pl.BlockSpec(memory_space=pl.ANY)


def lane_layout(start, freqs):
    lane = np.arange(WIDE)
    tail = lane >= 256
    imag = np.where(tail, lane >= 320, lane >= 128)
    freq = start + np.where(tail, 128 + lane % 64, lane % 128)
    return np.minimum(freq, freqs - 1), imag, freq < freqs


def row_tables(lon_len, start):
    freqs = lon_len // 2 + 1
    freq, imag, used = lane_layout(start, freqs)
    lon = np.arange(lon_len)
    turns = (lon[:, None] * freq[None, :] % lon_len).astype(np.float32) * np.float32(
        2.0 * math.pi / lon_len
    )
    scale = np.float32(1.0 / math.sqrt(lon_len))
    wave = np.where(imag, -np.sin(turns), np.cos(turns)) * used
    weight = np.where((freq == 0) | (freq == lon_len // 2), 1.0, 2.0).astype(np.float32)
    forward = (wave * scale).astype(ml_dtypes.bfloat16)
    inverse = (wave * weight * scale).astype(ml_dtypes.bfloat16)
    return forward.T, inverse


def guest_home(part):
    return part // 2 * 64 + part % 2 * GUEST


def guest_columns(table):
    guests = np.zeros((table.shape[0], 4 * LANES), table.dtype)
    for part in range(4):
        home = 2 * LANES + guest_home(part)
        width = min(GUEST, SPARE - part % 2 * GUEST)
        seat = part * LANES + SPARE
        guests[:, seat : seat + width] = table[:, home : home + width]
    return np.concatenate([table[:, : 2 * LANES], guests], axis=1)


def column_tables(spaces, rows, chan_part):
    lat_len = spaces * rows
    lat = np.arange(lat_len)
    turns = (lat[:, None] * lat[None, :] % lat_len).astype(np.float32) * np.float32(
        2.0 * math.pi / lat_len
    )
    scale = np.float32(1.0 / math.sqrt(lat_len))
    size = chan_part * lat_len
    order = lat.reshape(spaces, rows // 2, 2).transpose(1, 0, 2).reshape(-1)
    forward = np.zeros((chan_part, lat_len, 2, lat_len, chan_part), np.float32)
    for chan in range(chan_part):
        forward[chan, :, 0, :, chan] = (np.cos(turns) * scale)[:, order]
        forward[chan, :, 1, :, chan] = (np.sin(turns) * scale)[:, order]
    inverse = forward.transpose(3, 4, 2, 0, 1).reshape(size, 2 * size)
    forward = forward.reshape(size, 2 * size)
    return forward.astype(ml_dtypes.bfloat16), inverse.astype(ml_dtypes.bfloat16)


def swap_parts(values):
    tail = values[:, 2 * LANES :]
    return jnp.concatenate(
        [values[:, LANES : 2 * LANES], values[:, :LANES], pltpu.roll(tail, 64, axis=1)], axis=1
    )


def imag_lanes(shape):
    lane = lax.broadcasted_iota(jnp.int32, shape, len(shape) - 1)
    return ((lane >= LANES) & (lane < 2 * LANES)) | (lane >= 320)


def first_half(shape):
    return lax.broadcasted_iota(jnp.int32, shape, 1) < 4


def interleave(one, two):
    top = first_half(one.shape)
    return (
        jnp.where(top, one, pltpu.roll(two, 4, axis=1)),
        jnp.where(top, pltpu.roll(one, 4, axis=1), two),
    )


def normed_row(values, gain, bias):
    wide = values.astype(jnp.float32)
    center = jnp.mean(wide, axis=-1, keepdims=True)
    wide = wide - center
    spread = jnp.mean(jnp.square(wide), axis=-1, keepdims=True)
    return (wide * lax.rsqrt(spread + 1e-05) * gain + bias).astype(jnp.bfloat16)


def pair_spectra(x_ref, gain_ref, bias_ref, table):
    specs = []
    for row in range(2):
        normed = normed_row(x_ref[row], gain_ref[...], bias_ref[...])
        spec = jnp.dot(table, normed, preferred_element_type=jnp.float32).T
        specs.append(spec.reshape(spec.shape[0] // 8, 8, spec.shape[1]))
    return interleave(*specs)


def pre_kernel(x_ref, gain_ref, bias_ref, table_ref, out_ref):
    both = pair_spectra(x_ref, gain_ref, bias_ref, table_ref[...])
    for side in range(2):
        out_ref[:, side, 0] = both[side].astype(jnp.bfloat16)


def pre_packed_kernel(x_ref, gain_ref, bias_ref, table_ref, last_ref, out_ref):
    pair = pl.program_id(0)

    def main(both):
        for side in range(2):
            for tile in range(2):
                out_ref[:, side, 2 * pair + tile] = both[side][
                    :, :, tile * LANES : (tile + 1) * LANES
                ].astype(jnp.bfloat16)

    @pl.when(pair < PAIRS - 1)
    def _():
        both = pair_spectra(x_ref, gain_ref, bias_ref, table_ref[...])
        main(both)
        for side in range(2):
            out_ref[:, side, 2 * PAIRS + pair] = both[side][:, :, 2 * LANES :].astype(jnp.bfloat16)

    @pl.when(pair == PAIRS - 1)
    def _():
        both = pair_spectra(x_ref, gain_ref, bias_ref, last_ref[...])
        main(both)
        for side in range(2):
            for part in range(4):
                guest = both[side][:, :, (2 + part) * LANES : (3 + part) * LANES]
                tail = out_ref[:, side, 2 * PAIRS + part].astype(jnp.float32)
                out_ref[:, side, 2 * PAIRS + part] = (tail + guest).astype(jnp.bfloat16)


def pre(grid, gain, bias, table, packed):
    rows, lon_len, channels = grid.shape
    groups = channels // 8
    if packed:
        kernel = pre_packed_kernel
        shape = (groups, 2, 3 * PAIRS - 1, 8, LANES)
        out_spec = pl.BlockSpec(shape, lambda i: (0, 0, 0, 0, 0))
        tables = (table, guest_columns(table.T).T)
    else:
        kernel = pre_kernel
        shape = (groups, 2, PAIRS, 8, WIDE)
        out_spec = pl.BlockSpec((groups, 2, 1, 8, WIDE), lambda i: (0, 0, i, 0, 0))
        tables = (table,)
    out = pl.pallas_call(
        kernel,
        grid=(rows // 2,),
        in_specs=[
            pl.BlockSpec((2, lon_len, channels), lambda i: (i, 0, 0)),
            pl.BlockSpec((1, channels), lambda i: (0, 0)),
            pl.BlockSpec((1, channels), lambda i: (0, 0)),
        ]
        + [pl.BlockSpec(each.shape, lambda i: (0, 0)) for each in tables],
        out_specs=out_spec,
        out_shape=jax.ShapeDtypeStruct(shape, jnp.bfloat16),
        compiler_params=pltpu.CompilerParams(vmem_limit_bytes=VMEM),
        cost_estimate=pl.CostEstimate(
            flops=2 * rows * lon_len * channels * WIDE,
            bytes_accessed=2 * rows * channels * (lon_len + WIDE),
            transcendentals=rows * lon_len,
        ),
        name="row_forward",
    )(grid, gain, bias, *(jnp.asarray(each) for each in tables))
    return out.reshape(2 * groups, *shape[2:])


def guest_lanes(shape, first):
    lane = lax.broadcasted_iota(jnp.int32, shape, 1)
    return (lane >= first) & (lane < first + GUEST)


def load_pairs(x_ref, packed):
    pairs = []
    if not packed:
        for pair in range(PAIRS):
            rows = x_ref[:, pair].astype(jnp.float32)
            pairs.append(rows.reshape(rows.shape[0] * 8, WIDE))
        return pairs
    tiles = []
    for tile in range(3 * PAIRS - 1):
        rows = x_ref[:, tile].astype(jnp.float32)
        tiles.append(rows.reshape(rows.shape[0] * 8, LANES))
    tails = tiles[2 * PAIRS :]
    last = jnp.zeros_like(tails[0])
    for part in range(4):
        home = guest_home(part)
        moved = pltpu.roll(tails[part], (home - SPARE) % LANES, axis=1)
        last = jnp.where(guest_lanes(last.shape, home), moved, last)
    tails.append(last)
    for pair in range(PAIRS):
        pairs.append(jnp.concatenate([tiles[2 * pair], tiles[2 * pair + 1], tails[pair]], axis=1))
    return pairs


def store_pairs(out_ref, back, packed):
    count = back.shape[0] // PAIRS
    pairs = [back[pair * count : (pair + 1) * count] for pair in range(PAIRS)]
    if not packed:
        for pair in range(PAIRS):
            out_ref[:, pair] = pairs[pair].reshape(count // 8, 8, WIDE).astype(jnp.bfloat16)
        return
    tails = [rows[:, 2 * LANES :] for rows in pairs]
    for part in range(4):
        moved = pltpu.roll(tails[-1], (SPARE - guest_home(part)) % LANES, axis=1)
        tails[part] = jnp.where(guest_lanes(moved.shape, SPARE), moved, tails[part])
    tiles = []
    for rows in pairs:
        tiles += [rows[:, :LANES], rows[:, LANES : 2 * LANES]]
    for index, tile in enumerate(tiles + tails[:-1]):
        out_ref[:, index] = tile.reshape(count // 8, 8, LANES).astype(jnp.bfloat16)


def mid_kernel(packed, x_ref, filt_ref, forward_ref, inverse_ref, out_ref, x_both, mixed):
    size = x_both.shape[0] // 2
    count = size // PAIRS
    for pair, rows in enumerate(load_pairs(x_ref, packed)):
        turned = swap_parts(rows)
        x_both[pl.ds(pair * count, count)] = rows.astype(jnp.bfloat16)
        x_both[pl.ds(size + pair * count, count)] = jnp.where(
            imag_lanes(rows.shape), -turned, turned
        ).astype(jnp.bfloat16)
    lat_len = size // 4
    for chan in range(4):
        part = pl.ds(chan * lat_len, lat_len)
        spec = jnp.dot(forward_ref[part], x_both[...], preferred_element_type=jnp.float32)
        both = filt_ref[0, part] * spec + filt_ref[1, part] * swap_parts(spec)
        turned = swap_parts(both)
        mixed[part] = both.astype(jnp.bfloat16)
        mixed[pl.ds(size + chan * lat_len, lat_len)] = jnp.where(
            imag_lanes(both.shape), turned, -turned
        ).astype(jnp.bfloat16)
    back = jnp.dot(inverse_ref[...], mixed[...], preferred_element_type=jnp.float32)
    store_pairs(out_ref, back, packed)


def mid(slab, filt, forward, inverse, samples, packed):
    spaces = slab.shape[0] // samples
    size = forward.shape[0]
    block = pl.BlockSpec((spaces, *slab.shape[1:]), lambda s: (s, 0, 0, 0))
    once = pl.Buffered(1)
    return pl.pallas_call(
        functools.partial(mid_kernel, packed),
        grid=(samples,),
        in_specs=[
            block,
            pl.BlockSpec((2, size, WIDE), lambda s: (0, 0, 0), pipeline_mode=once),
            pl.BlockSpec((size, 2 * size), lambda s: (0, 0), pipeline_mode=once),
            pl.BlockSpec((size, 2 * size), lambda s: (0, 0), pipeline_mode=once),
        ],
        out_specs=block,
        out_shape=jax.ShapeDtypeStruct(slab.shape, jnp.bfloat16),
        scratch_shapes=[
            pltpu.VMEM((2 * size, WIDE), jnp.bfloat16),
            pltpu.VMEM((2 * size, WIDE), jnp.bfloat16),
        ],
        compiler_params=pltpu.CompilerParams(vmem_limit_bytes=VMEM),
        cost_estimate=pl.CostEstimate(
            flops=samples * 8 * size * size * WIDE,
            bytes_accessed=4 * samples * size * WIDE + 8 * size * (WIDE + size),
            transcendentals=0,
        ),
        name="columns",
    )(slab, filt, forward, inverse)


def post_kernel(packed, back_hbm, x_hbm, table_hbm, out_hbm, x_in, out, slab, spec, table, *sems):
    x_sem, out_sem, main_sem, tail_sem, table_sem = sems
    groups = slab.shape[0]
    tables = pltpu.make_async_copy(table_hbm, table, table_sem)

    def inputs(pair):
        mains = pl.ds(2 * pair, 2) if packed else pair
        copies = [
            pltpu.make_async_copy(
                back_hbm.at[:, :, mains], slab.at[:, :, mains], main_sem.at[pair]
            )
        ]
        if packed and pair < PAIRS - 1:
            tail = 2 * PAIRS + pair
            copies.append(
                pltpu.make_async_copy(
                    back_hbm.at[:, :, tail], slab.at[:, :, tail], tail_sem.at[pair]
                )
            )
        copies.append(
            pltpu.make_async_copy(x_hbm.at[pl.ds(2 * pair, 2)], x_in.at[pair], x_sem.at[pair])
        )
        return copies

    def output(pair):
        return pltpu.make_async_copy(out.at[pair], out_hbm.at[pl.ds(2 * pair, 2)], out_sem.at[pair])

    def rows_of(tile):
        both = (slab[:, side, tile].astype(jnp.float32) for side in range(2))
        return [each.reshape(groups * 8, each.shape[2]) for each in interleave(*both)]

    def tail_rows(pair):
        if pair < PAIRS - 1:
            return rows_of(2 * PAIRS + pair)
        last = [jnp.zeros((groups * 8, LANES), jnp.float32)] * 2
        for part in range(4):
            home = guest_home(part)
            for row, guest in enumerate(rows_of(2 * PAIRS + part)):
                moved = pltpu.roll(guest, (home - SPARE) % LANES, axis=1)
                last[row] = jnp.where(guest_lanes(moved.shape, home), moved, last[row])
        return last

    for copy in [tables] + inputs(0) + inputs(1):
        copy.start()
    for pair in range(PAIRS):
        for copy in inputs(pair):
            copy.wait()
        if pair == 0:
            tables.wait()
        if pair + 2 < PAIRS:
            for copy in inputs(pair + 2):
                copy.start()
        if packed:
            tiles = [rows_of(2 * pair), rows_of(2 * pair + 1), tail_rows(pair)]
        else:
            tiles = [rows_of(pair)]
        for row in range(2):
            lane = 0
            for tile in tiles:
                wide = tile[row].shape[1]
                spec[row, :, lane : lane + wide] = tile[row].astype(jnp.bfloat16)
                lane += wide
        for row in range(2):
            branch = lax.dot_general(
                table[...], spec[row], (((1,), (1,)), ((), ())), preferred_element_type=jnp.float32
            )
            out[pair, row] = (x_in[pair, row].astype(jnp.float32) + branch).astype(jnp.bfloat16)
        output(pair).start()
    for pair in range(PAIRS):
        output(pair).wait()


def post(back, grid, table, packed):
    rows, lon_len, channels = grid.shape
    groups = channels // 8
    back = back.reshape(groups, 2, *back.shape[1:])
    return pl.pallas_call(
        functools.partial(post_kernel, packed),
        in_specs=[ANY] * 3,
        out_specs=ANY,
        out_shape=jax.ShapeDtypeStruct(grid.shape, jnp.bfloat16),
        scratch_shapes=[
            pltpu.VMEM((PAIRS, 2, lon_len, channels), jnp.bfloat16),
            pltpu.VMEM((PAIRS, 2, lon_len, channels), jnp.bfloat16),
            pltpu.VMEM(back.shape, jnp.bfloat16),
            pltpu.VMEM((2, channels, WIDE), jnp.bfloat16),
            pltpu.VMEM((lon_len, WIDE), jnp.bfloat16),
        ]
        + [pltpu.SemaphoreType.DMA((PAIRS,))] * 4
        + [pltpu.SemaphoreType.DMA],
        compiler_params=pltpu.CompilerParams(vmem_limit_bytes=VMEM - MIB),
        cost_estimate=pl.CostEstimate(
            flops=2 * rows * lon_len * channels * WIDE,
            bytes_accessed=2 * rows * channels * (2 * lon_len + WIDE),
            transcendentals=0,
        ),
        name="row_inverse",
    )(back, grid, jnp.asarray(table))


def filter_chunk(filt, start):
    freqs = filt.shape[-1] // 2
    by_chan = filt.transpose(1, 0, 2).reshape(-1, 2 * freqs)

    def lanes(first):
        stop = min(start + HALF, freqs)
        taken = by_chan[:, first + start : first + stop]
        return jnp.pad(taken, ((0, 0), (0, HALF - taken.shape[1])))

    real, imag = lanes(0), lanes(freqs)

    def lay(one, two):
        return jnp.concatenate(
            [one[:, :LANES], two[:, :LANES], one[:, LANES:], two[:, LANES:]], axis=1
        )

    return jnp.stack([lay(real, real), lay(-imag, imag)])


def swap_devices(blocks):
    return lax.all_to_all(blocks, BOTH, split_axis=0, concat_axis=0, tiled=True)


def shards(samples, norm_gain, norm_bias, spectral_filter):
    grid = samples[0]
    rows, lon_len, _ = grid.shape
    dp_count = lax.axis_size("dp")
    starts = (0, HALF)
    tables = [row_tables(lon_len, start) for start in starts]
    columns = column_tables(lax.axis_size("space"), rows, spectral_filter.shape[1])
    forward, inverse = (jnp.asarray(each) for each in columns)
    gain, bias = norm_gain[None], norm_bias[None]
    spectra = [pre(grid, gain, bias, tables[index][0], index == 1) for index in range(2)]
    filts = [filter_chunk(spectral_filter, start) for start in starts]
    spectra[1], filts = lax.optimization_barrier((spectra[1], filts))
    slabs = [swap_devices(each) for each in spectra]
    backs = []
    for index in range(2):
        back = mid(slabs[index], filts[index], forward, inverse, dp_count, index == 1)
        backs.append(swap_devices(back))
    for index in range(2):
        grid = post(backs[index], grid, tables[index][1], index == 1)
    return grid[None]


def solution(mesh):
    placed = (P("dp", "space", None, None), P(), P(), P(None, BOTH, None))
    return jax.shard_map(
        shards, mesh=mesh, in_specs=placed, out_specs=P("dp", "space", None, None), check_vma=False
    )
```
